32 devices in a mesh: grp: 2 (over y), seq: 4 (over x, core), head: 4 (over z).
Axes of the slice: x: 2, y: 2, z: 4, core: 2. Of those that a mesh axis runs over, the one named last changes fastest.
Arguments:
- queries: bfloat16 [8192, 8192], P(('grp', 'seq'), 'head'), parts along dimension 0, may hold values from -4 to 4
- key_rows: bfloat16 [8192, 8192], P(('grp', 'seq'), 'head'), parts along dimension 0, may hold values from -4 to 4
- values: bfloat16 [8192, 8192], P(('grp', 'seq'), 'head'), parts along dimension 0, may hold values from -6 to 6
- decay_codes: int32 [64], P('head'), may hold values from 1 to 2047, as said below
- segment_ids: int32 [8192], P(('grp', 'seq')), parts along dimension 0, may hold values from 0 to 7, never falling along the last dimension, each value on 1 to 3072 neighbouring positions
- norm_gain: float32 [8192], P('head'), may hold values from 0.1 to 1.9
- out_weight: bfloat16 [8192, 6144], P('head', 'seq'), may hold values from -0.0625 to 0.0625
Outputs:
- mixed_tokens: bfloat16 [8192, 6144], P(('grp', 'seq', 'head')), parts along dimension 0
The draws below stay inside these ranges and needn't reach their ends.
There are 2 independent parts, one for each index of `grp`. The reference program is written for one: setup_inputs(seed, part) draws one part's arguments, and reference() takes and returns one part's arrays. A program takes and returns all parts, laid end to end along the dimension named above; an argument that names none is the same for every part. Nothing has to cross between parts.
Inputs may be any that keep to these rules, and one draw needn't show every extreme that they name: The decay of head h per position is 1 - decay_codes[h] / 65536. `segment_ids`: non-decreasing; each document is a run of 1 to min(3072, 4096) positions.
All inputs are finite; a program needn't handle non-finite values.
Results may differ from the reference program's by a relative error of at most 0.014.
Values may be sent and summed in bfloat16 or wider, within the bound.
No kernel may reach another device: no remote copies, remote signals or barrier semaphores. Data moves between devices by JAX's collectives and lax.ppermute only.
A program may use at most 192 MiB of HBM per device.

```python
import math
import jax
import jax.numpy as jnp
import numpy as np
from jax import lax

D = 6144
HEADS = 64
HEAD_DIM = 128
TOK_DEV = 1024
SPAN = 256
DOCS = 8
SEQ = 4096
HD = 8192
N_HEAD = 4


def draw_decay_codes(key, part):
    key = jax.random.fold_in(key, 7)
    key_exp, key_extra, key_top, key_low = jax.random.split(key, 4)
    exponent = jax.random.randint(key_exp, (HEADS,), 0, 11)
    lowest = jnp.left_shift(jnp.int32(1), exponent.astype(jnp.int32))
    surplus = jax.random.randint(key_extra, (HEADS,), 0, 1 << 30) % lowest
    codes = (lowest + surplus).astype(jnp.int32)
    top_head = jax.random.randint(key_top, (), 0, HEADS)
    low_head = (top_head + 1 + jax.random.randint(key_low, (), 0, HEADS - 1)) % HEADS
    places = jnp.arange(HEADS)
    codes = jnp.where(places == top_head, 2047, codes)
    codes = jnp.where(places == low_head, 1, codes)
    return codes.astype(jnp.int32)


def level_of(rng, extent, cuts, smallest, high):
    loudness = 1.0
    for dim, parts in cuts:
        heights = jax.random.uniform(jax.random.fold_in(jax.random.fold_in(rng, 6), dim), (parts,), jnp.float32, smallest / len(cuts), high / len(cuts))
        loudness = loudness * jnp.repeat(jnp.exp(heights), extent[dim] // parts).reshape((-1,) + (1,) * (len(extent) - 1 - dim))
    return loudness


def split_up(count, total, bound, skew):
    weights = [(1 << 20) // math.isqrt(grade ** skew) + 1 for grade in range(2, count + 1)]
    rest, counts = total - bound - (count - 1), [1] * (count - 1)
    while rest > 0:
        candidates = [i for i in range(count - 1) if counts[i] < bound]
        mass, left = sum([weights[i] for i in candidates]), rest
        for i in candidates:
            more = min(bound - counts[i], max(1, left * weights[i] // mass), rest)
            counts[i] = counts[i] + more
            rest = rest - more
    return np.array([bound] + counts)


def ragged(rng, count, total, bound, skew):
    if count == 2:
        one = jax.random.randint(rng, (), max(1, total - bound), min(bound, total - 1) + 1)
        return jnp.stack([one, total - one])
    lengths = jnp.asarray(split_up(count, total, bound, skew), jnp.int32)
    couples = (count - 1) // 2
    source_of, receiver = lengths[1:1 + 2 * couples:2], lengths[2:2 + 2 * couples:2]
    margin = jnp.minimum(source_of - 1, bound - receiver)
    shifted = jax.random.randint(jax.random.fold_in(rng, 1), (couples,), 0, 1 << 20) % (margin + 1)
    lengths = lengths.at[1:1 + 2 * couples:2].set(source_of - shifted).at[2:2 + 2 * couples:2].set(receiver + shifted)
    return lengths[jax.random.permutation(jax.random.fold_in(rng, 2), count)]


def gaussian(key, dims, deviation, reach, cuts=(), held_as=jnp.bfloat16):
    values = deviation * jax.random.normal(key, dims, jnp.float32)
    if cuts:
        values = values * level_of(key, dims, cuts, -0.22, 0.18)
    return jnp.clip(values, -reach, reach).astype(held_as)


def setup_inputs(seed: int = 0, part: int = 0) -> dict:
    streams_of = jax.random.split(jax.random.key(seed), 8)
    own_keys = jax.random.split(jax.random.fold_in(streams_of[7], part), 8)
    return {
        "queries": gaussian(own_keys[0], (SEQ, HD), 0.3, 4.0, ((0, 4), (1, 4))),
        "key_rows": gaussian(own_keys[1], (SEQ, HD), 0.3, 4.0, ((0, 4), (1, 4))),
        "values": gaussian(own_keys[2], (SEQ, HD), 1.0, 6.0, ((0, 4), (1, 4))),
        "decay_codes": draw_decay_codes(jax.random.fold_in(streams_of[7], 71), part),
        "segment_ids": jnp.searchsorted(jnp.cumsum(ragged(own_keys[4], DOCS, SEQ, min(3 * TOK_DEV, SEQ), 1)), jnp.arange(SEQ), side="right").astype(jnp.int32),
        "norm_gain": jnp.clip(1.0 + 0.18 * jax.random.normal(streams_of[5], (HD,), jnp.float32), 0.1, 1.9),
        "out_weight": gaussian(streams_of[6], (HD, D), HD ** -0.5, 0.0625, ((0, 4), (1, 4))),
    }


def lightning(query_all, key_all, value_all, seg_all, decay_log):
    length, heads_num, head_size = query_all.shape
    n_blocks = length // SPAN
    query_blocks = query_all.reshape(n_blocks, SPAN, heads_num, head_size)
    key_blocks = key_all.reshape(n_blocks, SPAN, heads_num, head_size)
    value_blocks = value_all.reshape(n_blocks, SPAN, heads_num, head_size)
    seg_blocks = seg_all.reshape(n_blocks, SPAN)
    offsets = jnp.arange(SPAN)
    distance = offsets[:, None] - offsets[None, :]
    causal = distance >= 0
    inner_decay = jnp.exp(jnp.where(causal, distance, 0).astype(jnp.float32)[None] * decay_log[:, None, None])
    head_decay = jnp.exp((offsets + 1).astype(jnp.float32)[:, None] * decay_log[None])
    tail_decay = jnp.exp((SPAN - 1 - offsets).astype(jnp.float32)[:, None] * decay_log[None])
    block_decay = jnp.exp(jnp.float32(SPAN) * decay_log)

    def advance(state_pair, block_in):
        memory, memory_seg = state_pair
        q_block, k_block, v_block, seg_block = block_in
        q_float = q_block.astype(jnp.float32)
        k_float = k_block.astype(jnp.float32)
        v_float = v_block.astype(jnp.float32)
        scores = jnp.einsum('thd,shd->hts', q_float, k_float)
        same_doc = causal & (seg_block[:, None] == seg_block[None, :])
        weights = jnp.where(same_doc[None], scores * inner_decay, 0.0).astype(jnp.bfloat16)
        inner = jnp.einsum('hts,she->the', weights.astype(jnp.float32), v_float)
        in_segment = (seg_block == memory_seg).astype(jnp.float32)
        earlier = jnp.einsum('thd,hde->the', q_float, memory, precision=lax.Precision.HIGHEST)
        earlier = earlier * (head_decay * in_segment[:, None])[:, :, None]
        last_seg = seg_block[-1]
        keep = (seg_block == last_seg).astype(jnp.float32)[:, None] * tail_decay
        added = jnp.einsum('shd,she->hde', k_float * keep[:, :, None], v_float, precision=lax.Precision.HIGHEST)
        carried = jnp.where(memory_seg == last_seg, block_decay, 0.0 * block_decay)
        memory = added + carried[:, None, None] * memory
        return ((memory, last_seg), inner + earlier)
    initial = (jnp.zeros((heads_num, head_size, head_size), jnp.float32), jnp.array(-1, jnp.int32))
    final_pair, results = lax.scan(advance, initial, (query_blocks, key_blocks, value_blocks, seg_blocks))
    return results.reshape(length, heads_num, head_size)

def reference(queries, key_rows, values, decay_codes, segment_ids, norm_gain, out_weight):
    decay_log = jnp.log1p(-decay_codes.astype(jnp.float32) / 65536.0)
    split_shape = (SEQ, HEADS, HEAD_DIM)
    attended = lightning(queries.reshape(split_shape), key_rows.reshape(split_shape), values.reshape(split_shape), segment_ids.astype(jnp.int32), decay_log)
    mean_square = lax.optimization_barrier(jnp.mean(attended * attended, axis=-1, keepdims=True))
    normed = attended * lax.rsqrt(mean_square + 1e-06) * norm_gain.reshape(HEADS, HEAD_DIM)
    normed = normed.astype(jnp.bfloat16).reshape(SEQ, HEADS * HEAD_DIM)
    group_width = HEADS * HEAD_DIM // N_HEAD
    running = jnp.zeros((SEQ, D), jnp.float32)
    for group_index in range(N_HEAD):
        lower = group_index * group_width
        partial_value = jnp.dot(normed[:, lower:lower + group_width], out_weight[lower:lower + group_width], preferred_element_type=jnp.float32).astype(jnp.bfloat16)
        partial_value = lax.optimization_barrier(partial_value)
        running = running + partial_value.astype(jnp.float32)
    return running.astype(jnp.bfloat16)
```

```python
import functools

import jax
import jax.numpy as jnp
from jax import lax
from jax.experimental import pallas as pl
from jax.experimental.pallas import tpu as pltpu
from jax.sharding import PartitionSpec as P

SPAN = 256
HEAD = 128
SEG_ROWS = 16
F32 = jnp.float32
BF16 = jnp.bfloat16


def iota(shape, dim):
    return lax.broadcasted_iota(jnp.int32, shape, dim)


def dot(a, b, dims):
    return lax.dot_general(a, b, (dims, ((), ())), preferred_element_type=F32)


def state_kernel(heads_step, decay_ref, keep_ref, seg_ref, k_ref, v_ref, out_ref):
    step = pl.program_id(0)
    tokens = k_ref.shape[0]
    heads = pl.num_programs(0) * heads_step

    @pl.when(step == 0)
    def _():
        out_ref[heads * HEAD:, :] = jnp.broadcast_to(seg_ref[...], (SEG_ROWS, HEAD)).astype(BF16)

    ahead = (tokens - 1 - iota((tokens, HEAD), 0)).astype(F32)
    for j in range(heads_step):
        head = step * heads_step + j
        cols = slice(j * HEAD, (j + 1) * HEAD)
        kept = k_ref[:, cols].astype(F32) * (jnp.exp(ahead * decay_ref[head]) * keep_ref[...])
        state = dot(kept.astype(BF16), v_ref[:, cols], ((0,), (0,)))
        out_ref[pl.ds(pl.multiple_of(head * HEAD, HEAD), HEAD), :] = state.astype(BF16)


def main_kernel(heads_step, decay_ref, carried_ref, mask_ref, inseg_ref, keep_ref, q_ref, k_ref, v_ref, out_ref):
    step = pl.program_id(0)
    blocks = q_ref.shape[0] // SPAN
    distance = jnp.maximum(iota((SPAN, SPAN), 0) - iota((SPAN, SPAN), 1), 0).astype(F32)
    place = iota((SPAN, HEAD), 0).astype(F32)
    for j in range(heads_step):
        decay = decay_ref[step * heads_step + j]
        cols = slice(j * HEAD, (j + 1) * HEAD)
        inner_decay = jnp.exp(distance * decay)
        head_decay = jnp.exp((place + 1.0) * decay)
        tail_decay = jnp.exp((SPAN - 1.0 - place) * decay)
        block_decay = jnp.exp(jnp.full((HEAD, HEAD), SPAN, F32) * decay)
        memory = None
        for b in range(blocks):
            rows = slice(b * SPAN, (b + 1) * SPAN)
            q, k, v = q_ref[rows, cols], k_ref[rows, cols], v_ref[rows, cols]
            scores = dot(q, k, ((1,), (1,)))
            weights = (scores * inner_decay * mask_ref[b]).astype(BF16)
            result = dot(weights, v, ((1,), (0,)))
            if b > 0:
                earlier = dot(q, memory.astype(BF16), ((1,), (0,)))
                result = result + earlier * (head_decay * inseg_ref[rows, :])
            out_ref[rows, cols] = result
            if b < blocks - 1:
                kept = (k.astype(F32) * (tail_decay * keep_ref[rows, :])).astype(BF16)
                added = dot(kept, v, ((0,), (0,)))
                memory = added if b == 0 else added + (block_decay * carried_ref[b]) * memory


def norm_kernel(heads, shards, scalar_ref, decay_ref, first_ref, infirst_ref, gain_ref, states_ref, q_ref, att_ref, out_ref, incoming):
    step = pl.program_id(0)
    rows = q_ref.shape[0]
    me = scalar_ref[0]
    tokens = scalar_ref[1]

    @pl.when(step == 0)
    def _():
        state_rows = heads * HEAD + SEG_ROWS
        active = []
        for s in range(shards - 1):
            seg = states_ref[s * state_rows + heads * HEAD:s * state_rows + heads * HEAD + 1, :].astype(F32)
            use = jnp.logical_and(seg == first_ref[...], s < me)
            active.append(jnp.where(use, 1.0, 0.0))
        for head in range(heads):
            total = jnp.zeros((HEAD, HEAD), F32)
            for s in range(shards - 1):
                gap = jnp.maximum(me - 1 - s, 0) * tokens
                factor = jnp.exp(jnp.full((1, HEAD), 1.0, F32) * gap.astype(F32) * decay_ref[head]) * active[s]
                base = s * state_rows + head * HEAD
                total = total + factor * states_ref[base:base + HEAD, :].astype(F32)
            incoming[head * HEAD:(head + 1) * HEAD, :] = total.astype(BF16)

    place = (iota((rows, HEAD), 0) + (step * rows + 1)).astype(F32)
    for head in range(heads):
        cols = slice(head * HEAD, (head + 1) * HEAD)
        before = dot(q_ref[:, cols], incoming[cols, :], ((1,), (0,)))
        att = att_ref[:, cols] + before * (jnp.exp(place * decay_ref[head]) * infirst_ref[...])
        square = jnp.mean(att * att, axis=-1, keepdims=True)
        out_ref[:, cols] = (att * lax.rsqrt(square + 1e-06) * gain_ref[:, cols]).astype(BF16)


def smem():
    return pl.BlockSpec(memory_space=pltpu.SMEM)


def whole(shape):
    return pl.BlockSpec(shape, lambda i: (0,) * len(shape))


def attention(queries, key_rows, values, decay_codes, segment_ids, norm_gain, my_index, shards):
    tokens, width = queries.shape
    heads = width // HEAD
    pair = 2
    decay_log = jnp.log1p(-decay_codes.astype(F32) / 65536.0)
    first_seg, last_seg = segment_ids[0], segment_ids[-1]
    spread = jnp.broadcast_to(segment_ids[:, None], (tokens, HEAD))
    seg_blocks = segment_ids.reshape(-1, SPAN)
    blocks = seg_blocks.shape[0]
    last_of = seg_blocks[:, -1]
    before_of = jnp.concatenate([jnp.full((1,), -1, jnp.int32), last_of[:-1]])
    by_row = lambda x: jnp.broadcast_to(x[:, None, None], (blocks, SPAN, HEAD)).reshape(tokens, HEAD)
    keep_all = (spread == last_seg).astype(F32)
    inseg = (spread == by_row(before_of)).astype(F32)
    keep = (spread == by_row(last_of)).astype(F32)
    carried = (before_of == last_of).astype(F32)
    offsets = jnp.arange(SPAN)
    causal = offsets[:, None] >= offsets[None, :]
    mask = (causal[None] & (seg_blocks[:, :, None] == seg_blocks[:, None, :])).astype(F32)
    infirst = (spread == first_seg).astype(F32)
    as_row = lambda x: jnp.broadcast_to(x.astype(F32)[None, None], (1, HEAD))

    column = lambda w: pl.BlockSpec((tokens, w), lambda i: (0, i))
    limit = pltpu.CompilerParams(vmem_limit_bytes=48 << 20)
    state_rows = heads * HEAD + SEG_ROWS
    wide = 4
    states = pl.pallas_call(
        functools.partial(state_kernel, wide),
        grid=(heads // wide,),
        in_specs=[smem(), whole((tokens, HEAD)), whole((1, HEAD)), column(wide * HEAD), column(wide * HEAD)],
        out_specs=whole((state_rows, HEAD)),
        out_shape=jax.ShapeDtypeStruct((state_rows, HEAD), BF16),
        compiler_params=limit,
        name="state",
    )(decay_log, keep_all, as_row(last_seg), key_rows, values)
    gathered = lax.all_gather(states, "seq", axis=0, tiled=True)
    attended = pl.pallas_call(
        functools.partial(main_kernel, pair),
        grid=(heads // pair,),
        in_specs=[smem(), smem(), whole(mask.shape), whole((tokens, HEAD)), whole((tokens, HEAD))]
        + [column(pair * HEAD)] * 3,
        out_specs=column(pair * HEAD),
        out_shape=jax.ShapeDtypeStruct((tokens, width), F32),
        compiler_params=limit,
        name="attend",
    )(decay_log, carried, mask, inseg, keep, queries, key_rows, values)
    rows = SPAN
    row_block = lambda w: pl.BlockSpec((rows, w), lambda i: (i, 0))
    return pl.pallas_call(
        functools.partial(norm_kernel, heads, shards),
        grid=(tokens // rows,),
        in_specs=[smem(), smem(), whole((1, HEAD)), row_block(HEAD), whole((1, width)), whole(gathered.shape),
                  row_block(width), row_block(width)],
        out_specs=row_block(width),
        out_shape=jax.ShapeDtypeStruct((tokens, width), BF16),
        scratch_shapes=[pltpu.VMEM((width, HEAD), BF16)],
        compiler_params=limit,
        name="norm",
    )(jnp.stack([my_index, jnp.int32(tokens)]).astype(jnp.int32), decay_log, as_row(first_seg), infirst,
      norm_gain[None], gathered, queries, attended)


def project(normed, weight):
    return jnp.dot(normed, weight, preferred_element_type=F32).astype(BF16)


def per_device(shards, queries, key_rows, values, decay_codes, segment_ids, norm_gain, out_weight):
    my_index = lax.axis_index("seq")
    quick = shards == 4
    if quick:
        sibling = [(0, 1), (1, 0), (2, 3), (3, 2)]
        across = [(0, 2), (2, 0), (1, 3), (3, 1)]
        near = lax.ppermute(out_weight, "seq", sibling)
        far = lax.ppermute(out_weight, "seq", across)
        far_near = lax.ppermute(far, "seq", sibling)
    normed = attention(queries, key_rows, values, decay_codes, segment_ids, norm_gain, my_index, shards)
    scatter = lambda x: lax.psum_scatter(x, "head", scatter_dimension=0, tiled=True)
    if not quick:
        return scatter(project(normed, lax.all_gather(out_weight, "seq", axis=1, tiled=True)))
    outs = [scatter(project(normed, w)) for w in (out_weight, near, far, far_near)]
    core, chip = my_index % 2, my_index // 2
    order = lambda flag, a, b: jnp.where(flag == 0, jnp.concatenate([a, b], 1), jnp.concatenate([b, a], 1))
    return order(chip, order(core, outs[0], outs[1]), order(core, outs[2], outs[3]))


def solution(mesh):
    in_specs = (
        P(("grp", "seq"), "head"),
        P(("grp", "seq"), "head"),
        P(("grp", "seq"), "head"),
        P("head"),
        P(("grp", "seq")),
        P("head"),
        P("head", "seq"),
    )
    out_specs = P(("grp", "seq", "head"), None)
    return jax.shard_map(
        functools.partial(per_device, mesh.shape["seq"]),
        mesh=mesh, in_specs=in_specs, out_specs=out_specs, check_vma=False,
    )
```

```python
import functools

import jax
import jax.numpy as jnp
from jax import lax
from jax.experimental import pallas as pl
from jax.experimental.pallas import tpu as pltpu
from jax.sharding import PartitionSpec as P

SPAN = 256
HEAD = 128
SEG_ROWS = 16
F32 = jnp.float32
BF16 = jnp.bfloat16
SCALE = 0.4


def cost(us):
    return pl.CostEstimate(flops=int(us * SCALE * 1.1535e9), bytes_accessed=1, transcendentals=0)


PARAMS = pltpu.CompilerParams(vmem_limit_bytes=48 << 20)


def iota(shape, dim):
    return lax.broadcasted_iota(jnp.int32, shape, dim)


def dot(a, b, dims=((1,), (0,))):
    return lax.dot_general(a, b, (dims, ((), ())), preferred_element_type=F32)


def ignore(kernel, inputs, extra):
    if not extra:
        return kernel
    return lambda *refs: kernel(*refs[:inputs], *refs[inputs + extra:])


def anywhere(extra):
    return [pl.BlockSpec(memory_space=pl.ANY)] * len(extra)


def smem():
    return pl.BlockSpec(memory_space=pltpu.SMEM)


def whole(shape):
    return pl.BlockSpec(shape, lambda *i: (0,) * len(shape))


def state_kernel(heads_step, decay_ref, seg_ref, k_ref, v_ref, out_ref):
    step = pl.program_id(0)
    tokens = k_ref.shape[0]
    heads = pl.num_programs(0) * heads_step
    segs = seg_ref[...]
    last = segs[segs.shape[0] - 1:, HEAD - 1:]
    start = tokens - jnp.sum((segs == last).astype(jnp.int32))

    @pl.when(step == 0)
    def _():
        out_ref[heads * HEAD:, :] = jnp.broadcast_to(last.astype(F32), (SEG_ROWS, HEAD)).astype(BF16)

    place = iota((tokens, HEAD), 0)
    ahead = (tokens - 1 - place).astype(F32)
    kept_rows = place >= start
    for j in range(heads_step):
        head = step * heads_step + j
        cols = slice(j * HEAD, (j + 1) * HEAD)
        kept = jnp.where(kept_rows, k_ref[:, cols].astype(F32) * jnp.exp(ahead * decay_ref[head]), 0.0)
        state = dot(kept.astype(BF16), v_ref[:, cols], ((0,), (0,)))
        out_ref[pl.ds(pl.multiple_of(head * HEAD, HEAD), HEAD), :] = state.astype(BF16)


def main_kernel(heads_step, decay_ref, row_ref, q_ref, k_ref, v_ref, out_ref, mask, bounds):
    step = pl.program_id(0)
    blocks = q_ref.shape[0] // SPAN

    @pl.when(step == 0)
    def _():
        before = jnp.full((1, 1), -1, jnp.int32)
        causal = iota((SPAN, SPAN), 0) >= iota((SPAN, SPAN), 1)
        for b in range(blocks):
            row = row_ref[:, b * SPAN:(b + 1) * SPAN]
            across = jnp.broadcast_to(row, (SPAN, SPAN)).astype(F32)
            same = jnp.logical_and(causal, across == across.T)
            mask[b] = jnp.where(same, 1.0, 0.0)
            last = row[:, SPAN - 1:]
            bounds[0, b] = jnp.sum((row == before).astype(jnp.int32))
            bounds[1, b] = SPAN - jnp.sum((row == last).astype(jnp.int32))
            bounds[2, b] = jnp.sum((last == before).astype(jnp.int32))
            before = last

    distance = jnp.maximum(iota((SPAN, SPAN), 0) - iota((SPAN, SPAN), 1), 0).astype(F32)
    place = iota((SPAN, HEAD), 0)
    count = place.astype(F32)
    for j in range(heads_step):
        decay = decay_ref[step * heads_step + j]
        cols = slice(j * HEAD, (j + 1) * HEAD)
        inner_decay = jnp.exp(distance * decay)
        head_decay = jnp.exp((count + 1.0) * decay)
        tail_decay = jnp.exp((SPAN - 1.0 - count) * decay)
        block_decay = jnp.exp(jnp.full((HEAD, HEAD), SPAN, F32) * decay)
        memory = None
        for b in range(blocks):
            rows = slice(b * SPAN, (b + 1) * SPAN)
            q, k, v = q_ref[rows, cols], k_ref[rows, cols], v_ref[rows, cols]
            weights = (dot(q, k, ((1,), (1,))) * inner_decay * mask[b]).astype(BF16)
            result = dot(weights, v)
            if b > 0:
                earlier = dot(q, memory.astype(BF16))
                result = result + jnp.where(place < bounds[0, b], earlier * head_decay, 0.0)
            out_ref[rows, cols] = result
            if b < blocks - 1:
                kept = jnp.where(place >= bounds[1, b], k.astype(F32) * tail_decay, 0.0).astype(BF16)
                added = dot(kept, v, ((0,), (0,)))
                if b > 0:
                    added = added + jnp.where(bounds[2, b] > 0, block_decay * memory, 0.0)
                memory = added


def incoming_kernel(me_ref, decay_ref, seg_ref, *refs):
    states, out_ref = refs[:-1], refs[-1]
    me, tokens = me_ref[0], me_ref[1]
    heads = out_ref.shape[0] // HEAD
    first = seg_ref[0:1, 0:1].astype(F32)
    active = []
    for s, ref in enumerate(states):
        seg = ref[heads * HEAD:heads * HEAD + 1, :].astype(F32)
        active.append(jnp.where(jnp.logical_and(seg == first, me_ref[2 + s] < me), 1.0, 0.0))
    for head in range(heads):
        rows = slice(head * HEAD, (head + 1) * HEAD)
        total = jnp.zeros((HEAD, HEAD), F32)
        for s, ref in enumerate(states):
            gap = jnp.maximum(me - 1 - me_ref[2 + s], 0) * tokens
            factor = jnp.exp(jnp.full((1, HEAD), 1.0, F32) * gap.astype(F32) * decay_ref[head]) * active[s]
            total = total + factor * ref[rows, :].astype(F32)
        out_ref[rows, :] = total.astype(BF16)


def norm_kernel(order, tiles, block_ref, decay_ref, seg_ref, gain_ref, incoming_ref, q_ref, att_ref, out_ref):
    rows, width = q_ref.shape
    start = block_ref[order] * (rows * tiles) + pl.program_id(0) * rows
    segs = seg_ref[...]
    carried_rows = jnp.sum((segs == segs[0:1, 0:1]).astype(jnp.int32))
    place = iota((rows, HEAD), 0) + start
    count = (place + 1).astype(F32)
    reached = place < carried_rows
    for head in range(width // HEAD):
        cols = slice(head * HEAD, (head + 1) * HEAD)
        before = dot(q_ref[:, cols], incoming_ref[cols, :])
        att = att_ref[:, cols] + jnp.where(reached, before * jnp.exp(count * decay_ref[head]), 0.0)
        square = jnp.mean(att * att, axis=-1, keepdims=True)
        out_ref[:, cols] = (att * lax.rsqrt(square + 1e-06) * gain_ref[:, cols]).astype(BF16)


def shard_state(decay_log, segs, key_rows, values):
    tokens, width = key_rows.shape
    wide = min(4, width // HEAD)
    column = pl.BlockSpec((tokens, wide * HEAD), lambda i: (0, i))
    return pl.pallas_call(
        functools.partial(state_kernel, wide),
        grid=(width // (wide * HEAD),),
        in_specs=[smem(), whole(segs.shape), column, column],
        out_specs=whole((width + SEG_ROWS, HEAD)),
        out_shape=jax.ShapeDtypeStruct((width + SEG_ROWS, HEAD), BF16),
        compiler_params=PARAMS, cost_estimate=cost(6), name="state",
    )(decay_log, segs, key_rows, values)


def attend(decay_log, segment_ids, queries, key_rows, values, after=()):
    tokens, width = queries.shape
    wide = 2
    column = pl.BlockSpec((tokens, wide * HEAD), lambda i: (0, i))
    return pl.pallas_call(
        ignore(functools.partial(main_kernel, wide), 5, len(after)),
        grid=(width // (wide * HEAD),),
        in_specs=[smem(), whole((1, tokens))] + [column] * 3 + anywhere(after),
        out_specs=column,
        out_shape=jax.ShapeDtypeStruct((tokens, width), F32),
        scratch_shapes=[pltpu.VMEM((tokens // SPAN, SPAN, SPAN), F32), pltpu.SMEM((3, tokens // SPAN), jnp.int32)],
        compiler_params=PARAMS, cost_estimate=cost(14), name="attend",
    )(decay_log, segment_ids.reshape(1, tokens), queries, key_rows, values, *after)


def incoming_state(my_index, tokens, decay_log, segs, width, states, owners, after=()):
    numbers = jnp.stack([my_index, jnp.int32(tokens)] + [jnp.int32(0) + o for o in owners]).astype(jnp.int32)
    vmem = pl.BlockSpec(memory_space=pltpu.VMEM)
    return pl.pallas_call(
        ignore(incoming_kernel, 3 + len(states), len(after)),
        in_specs=[smem(), smem()] + [vmem] * (1 + len(states)) + anywhere(after),
        out_specs=vmem,
        out_shape=jax.ShapeDtypeStruct((width, HEAD), BF16),
        compiler_params=PARAMS, cost_estimate=cost(1.5), name="incoming",
    )(numbers, decay_log, segs, *states, *after)


def normed(places, order, decay_log, segs, gain, incoming, queries, attended, after=()):
    tokens, width = queries.shape
    part = tokens // places.shape[0]
    tiles = 2
    rows = part // tiles
    at = lambda w: pl.BlockSpec((rows, w), lambda i, block: (block[order] * tiles + i, 0))
    return pl.pallas_call(
        ignore(functools.partial(norm_kernel, order, tiles), 7, len(after)),
        grid_spec=pltpu.PrefetchScalarGridSpec(
            num_scalar_prefetch=1,
            grid=(tiles,),
            in_specs=[smem(), whole(segs.shape), whole((1, width)), whole((width, HEAD)), at(width), at(width)] + anywhere(after),
            out_specs=pl.BlockSpec((rows, width), lambda i, block: (i, 0)),
        ),
        out_shape=jax.ShapeDtypeStruct((part, width), BF16),
        compiler_params=PARAMS, cost_estimate=cost(3.2), name="norm",
    )(places, decay_log, segs, gain, incoming, queries, attended, *after)


def product_kernel(jobs, inputs, off_ref, *refs):
    rows, weights, outs = refs[:inputs], refs[inputs:inputs + 2], refs[inputs + 2:]
    for (row, side), out in zip(jobs, outs):
        weight = weights[side][...] if len(weights[side].shape) == 2 else weights[side][0]
        out[...] = dot(rows[row][...], weight).astype(out.dtype)


def product_us(jobs, wide):
    return 2.0 + 0.9 * len(jobs) * wide / 512


def product(offsets, jobs, dtypes, rows, weights, after=()):
    size, depth = rows[0].shape
    gathered = len(weights[0].shape) == 3
    if gathered:
        wide = weights[0].shape[2]
        slices = weights[0].shape[0] // 2
        spec = lambda side: pl.BlockSpec((1, depth, wide), lambda j, off: (j * slices + off[side], 0, 0))
        steps = 2
    else:
        wide = 256
        steps = weights[0].shape[1] // wide
        spec = lambda side: pl.BlockSpec((depth, wide), lambda j, off: (0, j))
    return pl.pallas_call(
        ignore(functools.partial(product_kernel, jobs, len(rows)), 3 + len(rows), len(after)),
        grid_spec=pltpu.PrefetchScalarGridSpec(
            num_scalar_prefetch=1,
            grid=(steps,),
            in_specs=[whole((size, depth))] * len(rows) + [spec(0), spec(1)] + anywhere(after),
            out_specs=[pl.BlockSpec((size, wide), lambda j, off: (0, j))] * len(jobs),
        ),
        out_shape=[jax.ShapeDtypeStruct((size, steps * wide), d) for d in dtypes],
        compiler_params=PARAMS, cost_estimate=cost(product_us(jobs, steps * wide)), name="product",
    )(offsets, *rows, *weights, *after)


def plain(shards, queries, key_rows, values, decay_codes, segment_ids, norm_gain, out_weight):
    tokens, width = queries.shape
    me = lax.axis_index("seq")
    decay_log = jnp.log1p(-decay_codes.astype(F32) / 65536.0)
    segs = segment_ids.reshape(-1, HEAD)
    gathered = lax.all_gather(shard_state(decay_log, segs, key_rows, values), "seq", axis=0)
    attended = attend(decay_log, segment_ids, queries, key_rows, values)
    incoming = incoming_state(me, tokens, decay_log, segs, width, [gathered[s] for s in range(shards - 1)], range(shards - 1))
    places = jnp.zeros((1,), jnp.int32)
    rows = normed(places, 0, decay_log, segs, norm_gain[None], incoming, queries, attended)
    weight = lax.all_gather(out_weight, "seq", axis=1, tiled=True)
    partials = jnp.dot(rows, weight, preferred_element_type=F32)
    return lax.psum_scatter(partials.astype(BF16), "head", scatter_dimension=0, tiled=True)


def finish_kernel(half, off_ref, left, left_back, left_own, right, right_back, right_own, _, out):
    step = pl.program_id(0)

    @pl.when(step < half)
    def _():
        out[...] = (left[...].astype(F32) + left_back[...].astype(F32) + left_own[...]).astype(out.dtype)

    @pl.when(step >= half)
    def _():
        out[...] = (right[...].astype(F32) + right_back[...].astype(F32) + right_own[...]).astype(out.dtype)


def finish(spots, lefts, rights, out, after=()):
    rows, wide = lefts[0].shape
    half = wide // 256
    early = pl.BlockSpec((rows, 256), lambda j, off: (0, jnp.minimum(j, half - 1)))
    late = pl.BlockSpec((rows, 256), lambda j, off: (0, jnp.maximum(j, half) - half))
    return pl.pallas_call(
        ignore(functools.partial(finish_kernel, half), 8, len(after)),
        grid_spec=pltpu.PrefetchScalarGridSpec(
            num_scalar_prefetch=1,
            grid=(2 * half,),
            in_specs=[early] * 3 + [late] * 3 + [pl.BlockSpec(memory_space=pl.ANY)] + anywhere(after),
            out_specs=pl.BlockSpec((rows, 256), lambda j, off: (0, off[j])),
        ),
        out_shape=jax.ShapeDtypeStruct(out.shape, out.dtype),
        input_output_aliases={7: 0},
        compiler_params=PARAMS, cost_estimate=cost(2), name="finish",
    )(spots, *lefts, *rights, out, *after)


def merge_kernel(a, b, c, d, left, right):
    left[...] = (a[...].astype(F32) + b[...]).astype(BF16)
    right[...] = (c[...].astype(F32) + d[...]).astype(BF16)


def merge(came, own, came_back, own_back, after=()):
    rows, wide = came.shape
    part = pl.BlockSpec((rows, 512), lambda j: (0, j))
    shape = jax.ShapeDtypeStruct(came.shape, BF16)
    return pl.pallas_call(
        ignore(merge_kernel, 4, len(after)),
        grid=(wide // 512,),
        in_specs=[part] * 4 + anywhere(after),
        out_specs=[part] * 2,
        out_shape=[shape, shape],
        compiler_params=PARAMS, cost_estimate=cost(1.5), name="merge",
    )(came, own, came_back, own_back, *after)


def cut_kernel(off_ref, x_ref, out_ref):
    out_ref[...] = x_ref[...]


def cut(starts, which, wide, weight, after=()):
    depth = weight.shape[0]
    return pl.pallas_call(
        ignore(cut_kernel, 2, len(after)),
        grid_spec=pltpu.PrefetchScalarGridSpec(
            num_scalar_prefetch=1,
            grid=(wide // 256,),
            in_specs=[pl.BlockSpec((depth, 256), lambda j, off: (0, off[which] + j))] + anywhere(after),
            out_specs=pl.BlockSpec((depth, 256), lambda j, off: (0, j)),
        ),
        out_shape=jax.ShapeDtypeStruct((depth, wide), weight.dtype),
        compiler_params=PARAMS, cost_estimate=cost(2), name="cut",
    )(starts, weight, *after)


def pass_kernel(x_ref, out_ref):
    out_ref[...] = x_ref[...]


def passed(x, after):
    return pl.pallas_call(
        ignore(pass_kernel, 1, len(after)),
        grid=(1,),
        in_specs=[whole(x.shape)] + anywhere(after),
        out_specs=whole(x.shape),
        out_shape=jax.ShapeDtypeStruct(x.shape, x.dtype),
        compiler_params=PARAMS, cost_estimate=cost(1), name="pass",
    )(x, *after)


def ringed(queries, key_rows, values, decay_codes, segment_ids, norm_gain, out_weight):
    tokens, width = queries.shape
    me, line, copy = lax.axis_index("seq"), lax.axis_index("head"), lax.axis_index("grp")
    core, chip = me % 2, me // 2
    ways = [lambda x, d=d: lax.ppermute(x, "head", [(i, (i + d) % 4) for i in range(4)]) for d in (1, 3)]
    sibling = lambda x: lax.ppermute(x, "seq", [(0, 1), (1, 0), (2, 3), (3, 2)])
    onward = lambda x: lax.ppermute(x, "seq", [(0, 2), (1, 3)])
    gather = lambda x: lax.all_gather(x, ("grp", "seq"), axis=0)

    depth, columns = out_weight.shape
    half = columns // 2
    cuts = [(0, half // 3 * 2), (half // 3 * 2, half)]
    decay_log = jnp.log1p(-decay_codes.astype(F32) / 65536.0)
    segs = segment_ids.reshape(-1, HEAD)
    gain = norm_gain[None]
    places = jnp.stack([(line + b) % 4 for b in range(4)]).astype(jnp.int32)
    slices = [chip * 2 + core, chip * 2 + 1 - core, (1 - chip) * 2 + core, (1 - chip) * 2 + 1 - core]
    far_offsets = jnp.stack(slices[2:]).astype(jnp.int32)
    starts = jnp.stack([copy * (half // 256) + low // 256 for low, _ in cuts]).astype(jnp.int32)

    near = sibling(out_weight)
    state = shard_state(decay_log, segs, key_rows, values)
    state_x, state_c = onward(state), sibling(state)
    attended = attend(decay_log, segment_ids, queries, key_rows, values, after=[state])
    state_x = passed(state_x, [attended])
    state_d = sibling(state_x)
    pieces = [cut(starts, i, high - low, out_weight, after=[state_x]) for i, (low, high) in enumerate(cuts)]
    far = [gather(x) for x in pieces]
    owners = [jnp.where(core == 1, me - 1, 4), jnp.where(me >= 2, me - 2, 4), jnp.where(me >= 2, 1 - core, 4)]
    incoming = incoming_state(me, tokens, decay_log, segs, width, [state_c, state_x, state_d], owners, after=pieces)
    norm = lambda i, *after: normed(places, i, decay_log, segs, gain, incoming, queries, attended, after=after)

    chunks = [(slices[:2], [out_weight, near], list(range(columns // 256)))]
    for (low, high), x in zip(cuts, far):
        chunks.append((slices[2:], [x] * 2, [t * (half // 256) + i for t in range(2) for i in range(low // 256, high // 256)]))
    rows = {2: norm(2)}
    out = jnp.zeros((SPAN, 4 * columns), BF16)
    last, waiting = rows[2], None
    for owners, pair, tiles in chunks:
        def mul(jobs, dtypes, *after):
            used = sorted({r for r, _ in jobs})
            where = [(used.index(r), side) for r, side in jobs]
            return product(far_offsets, where, dtypes, [rows[r] for r in used], pair, after=after)

        across = mul([(2, 0), (2, 1)], [BF16] * 2, last)
        come = [way(x) for way, x in zip(ways, across)]
        if 1 not in rows:
            rows[1] = norm(1, across[0])
            rows[3] = norm(3, rows[1])
        left, right, *mine = mul([(3, 0), (1, 1), (1, 0), (3, 1)], [BF16, BF16, F32, F32], across[0])
        straight = [ways[1](left), ways[0](right)]
        if 0 not in rows:
            rows[0] = norm(0, left)
        own = mul([(0, 0), (0, 1)], [F32] * 2, left)
        if waiting is not None:
            out = waiting(out, own[0])
        sums = merge(come[0], mine[0], come[1], mine[1], after=[own[0], out])
        last = sums[0]
        sums = [way(x) for way, x in zip(ways, sums)]
        spots = jnp.stack([owner * (columns // 256) + tile for owner in owners for tile in tiles]).astype(jnp.int32)

        def waiting(out, after, spots=spots, sums=sums, straight=straight, own=own):
            return finish(spots, [sums[0], straight[0], own[0]], [straight[1], sums[1], own[1]], out, after=[after])

    return waiting(out, last)


def per_device(sizes, *args):
    if sizes == (2, 4, 4) and args[-1].shape[1] == 1536:
        return ringed(*args)
    return plain(sizes[1], *args)


def solution(mesh):
    in_specs = (
        P(("grp", "seq"), "head"),
        P(("grp", "seq"), "head"),
        P(("grp", "seq"), "head"),
        P("head"),
        P(("grp", "seq")),
        P("head"),
        P("head", "seq"),
    )
    out_specs = P(("grp", "seq", "head"), None)
    sizes = (mesh.shape["grp"], mesh.shape["seq"], mesh.shape["head"])
    return jax.shard_map(
        functools.partial(per_device, sizes), mesh=mesh, in_specs=in_specs, out_specs=out_specs, check_vma=False
    )
```

```python
import functools

import jax
import jax.numpy as jnp
from jax import lax
from jax.experimental import pallas as pl
from jax.experimental.pallas import tpu as pltpu
from jax.sharding import PartitionSpec as P

SPAN = 256
HEAD = 128
SEG_ROWS = 16
F32 = jnp.float32
BF16 = jnp.bfloat16
SCALE = 0.02


def cost(us):
    return pl.CostEstimate(flops=int(us * SCALE * 1.1535e9), bytes_accessed=1, transcendentals=0)


PARAMS = pltpu.CompilerParams(vmem_limit_bytes=48 << 20)


def iota(shape, dim):
    return lax.broadcasted_iota(jnp.int32, shape, dim)


def dot(a, b, dims=((1,), (0,))):
    return lax.dot_general(a, b, (dims, ((), ())), preferred_element_type=F32)


def ignore(kernel, inputs, extra):
    if not extra:
        return kernel
    return lambda *refs: kernel(*refs[:inputs], *refs[inputs + extra:])


def anywhere(extra):
    return [pl.BlockSpec(memory_space=pl.ANY)] * len(extra)


def smem():
    return pl.BlockSpec(memory_space=pltpu.SMEM)


def whole(shape):
    return pl.BlockSpec(shape, lambda *i: (0,) * len(shape))


def block_bounds(row, before):
    last = row[:, SPAN - 1:]
    continued = jnp.sum((row == before).astype(jnp.int32))
    start = SPAN - jnp.sum((row == last).astype(jnp.int32))
    return continued, start, jnp.sum((last == before).astype(jnp.int32)), last


def state_kernel(heads_step, decay_ref, row_ref, k_ref, v_ref, prefix_ref, out_ref, bounds):
    step = pl.program_id(0)
    blocks = k_ref.shape[0] // SPAN
    heads = pl.num_programs(0) * heads_step

    @pl.when(step == 0)
    def _():
        before = jnp.full((1, 1), -1, jnp.int32)
        for b in range(blocks):
            _, bounds[0, b], bounds[1, b], before = block_bounds(row_ref[b:b + 1, :], before)
        out_ref[heads * HEAD:, :] = jnp.broadcast_to(before.astype(F32), (SEG_ROWS, HEAD)).astype(BF16)

    place = iota((SPAN, HEAD), 0)
    count = place.astype(F32)
    for j in range(heads_step):
        head = step * heads_step + j
        cols = slice(j * HEAD, (j + 1) * HEAD)
        rows_out = pl.ds(pl.multiple_of(head * HEAD, HEAD), HEAD)
        tail_decay = jnp.exp((SPAN - 1.0 - count) * decay_ref[head])
        block_decay = jnp.exp(jnp.full((HEAD, HEAD), SPAN, F32) * decay_ref[head])
        memory = jnp.zeros((HEAD, HEAD), F32)
        for b in range(blocks):
            rows = slice(b * SPAN, (b + 1) * SPAN)
            prefix_ref[b, rows_out, :] = memory.astype(BF16)
            kept = jnp.where(place >= bounds[0, b], k_ref[rows, cols].astype(F32) * tail_decay, 0.0).astype(BF16)
            added = dot(kept, v_ref[rows, cols], ((0,), (0,)))
            memory = added + jnp.where(bounds[1, b] > 0, block_decay * memory, 0.0)
        out_ref[rows_out, :] = memory.astype(BF16)


def block_kernel(order, heads_step, block_ref, decay_ref, row_ref, gain_ref, incoming_ref, prefix_ref, q_ref, k_ref, v_ref, out_ref,
                 mask, bounds):
    step = pl.program_id(0)
    block = block_ref[order]

    @pl.when(step == 0)
    def _():
        row = row_ref[pl.ds(block, 1), :]
        earlier = row_ref[pl.ds(jnp.maximum(block - 1, 0), 1), :][:, SPAN - 1:]
        bounds[0], _, _, _ = block_bounds(row, jnp.where(block > 0, earlier, -1))
        bounds[1] = jnp.sum((row == row_ref[0:1, 0:1]).astype(jnp.int32))
        across = jnp.broadcast_to(row, (SPAN, SPAN)).astype(F32)
        same = jnp.logical_and(iota((SPAN, SPAN), 0) >= iota((SPAN, SPAN), 1), across == across.T)
        mask[...] = jnp.where(same, 1.0, 0.0)

    distance = jnp.maximum(iota((SPAN, SPAN), 0) - iota((SPAN, SPAN), 1), 0).astype(F32)
    place = iota((SPAN, HEAD), 0)
    count = (place + 1).astype(F32)
    from_start = count + (block * SPAN).astype(F32)
    for j in range(heads_step):
        decay = decay_ref[step * heads_step + j]
        cols = slice(j * HEAD, (j + 1) * HEAD)
        q, v = q_ref[:, cols], v_ref[:, cols]
        weights = (dot(q, k_ref[:, cols], ((1,), (1,))) * jnp.exp(distance * decay) * mask[...]).astype(BF16)
        att = dot(weights, v)
        att = att + jnp.where(place < bounds[0], dot(q, prefix_ref[0, cols, :]) * jnp.exp(count * decay), 0.0)
        att = att + jnp.where(place < bounds[1], dot(q, incoming_ref[cols, :]) * jnp.exp(from_start * decay), 0.0)
        square = jnp.mean(att * att, axis=-1, keepdims=True)
        out_ref[:, cols] = (att * lax.rsqrt(square + 1e-06) * gain_ref[:, cols]).astype(BF16)


def incoming_kernel(me_ref, decay_ref, seg_ref, *refs):
    states, out_ref = refs[:-1], refs[-1]
    me, tokens = me_ref[0], me_ref[1]
    heads = out_ref.shape[0] // HEAD
    first = seg_ref[0:1, 0:1].astype(F32)
    active = []
    for s, ref in enumerate(states):
        seg = ref[heads * HEAD:heads * HEAD + 1, :].astype(F32)
        active.append(jnp.where(jnp.logical_and(seg == first, me_ref[2 + s] < me), 1.0, 0.0))
    for head in range(heads):
        rows = slice(head * HEAD, (head + 1) * HEAD)
        total = jnp.zeros((HEAD, HEAD), F32)
        for s, ref in enumerate(states):
            gap = jnp.maximum(me - 1 - me_ref[2 + s], 0) * tokens
            factor = jnp.exp(jnp.full((1, HEAD), 1.0, F32) * gap.astype(F32) * decay_ref[head]) * active[s]
            total = total + factor * ref[rows, :].astype(F32)
        out_ref[rows, :] = total.astype(BF16)


def shard_state(decay_log, segs, key_rows, values):
    tokens, width = key_rows.shape
    wide = min(4, width // HEAD)
    blocks = tokens // SPAN
    column = pl.BlockSpec((tokens, wide * HEAD), lambda i: (0, i))
    shapes = [(blocks, width, HEAD), (width + SEG_ROWS, HEAD)]
    return pl.pallas_call(
        functools.partial(state_kernel, wide),
        grid=(width // (wide * HEAD),),
        in_specs=[smem(), whole(segs.shape), column, column],
        out_specs=[whole(x) for x in shapes],
        out_shape=[jax.ShapeDtypeStruct(x, BF16) for x in shapes],
        scratch_shapes=[pltpu.SMEM((2, blocks), jnp.int32)],
        compiler_params=PARAMS, cost_estimate=cost(6), name="state",
    )(decay_log, segs, key_rows, values)


def incoming_state(my_index, tokens, decay_log, segs, width, states, owners, after=()):
    numbers = jnp.stack([my_index, jnp.int32(tokens)] + [jnp.int32(0) + o for o in owners]).astype(jnp.int32)
    vmem = pl.BlockSpec(memory_space=pltpu.VMEM)
    return pl.pallas_call(
        ignore(incoming_kernel, 3 + len(states), len(after)),
        in_specs=[smem(), smem()] + [vmem] * (1 + len(states)) + anywhere(after),
        out_specs=vmem,
        out_shape=jax.ShapeDtypeStruct((width, HEAD), BF16),
        compiler_params=PARAMS, cost_estimate=cost(1.5), name="incoming",
    )(numbers, decay_log, segs, *states, *after)


def normed(places, order, decay_log, segs, gain, incoming, prefix, queries, key_rows, values, after=()):
    tokens, width = queries.shape
    wide = min(4, width // HEAD)
    at = pl.BlockSpec((SPAN, wide * HEAD), lambda i, block: (block[order], i))
    states = pl.BlockSpec((wide * HEAD, HEAD), lambda i, block: (i, 0))
    before = pl.BlockSpec((1, wide * HEAD, HEAD), lambda i, block: (block[order], i, 0))
    return pl.pallas_call(
        ignore(functools.partial(block_kernel, order, wide), 9, len(after)),
        grid_spec=pltpu.PrefetchScalarGridSpec(
            num_scalar_prefetch=1,
            grid=(width // (wide * HEAD),),
            in_specs=[smem(), whole(segs.shape), pl.BlockSpec((1, wide * HEAD), lambda i, block: (0, i)), states, before, at, at, at]
            + anywhere(after),
            out_specs=pl.BlockSpec((SPAN, wide * HEAD), lambda i, block: (0, i)),
            scratch_shapes=[pltpu.VMEM((SPAN, SPAN), F32), pltpu.SMEM((2,), jnp.int32)],
        ),
        out_shape=jax.ShapeDtypeStruct((SPAN, width), BF16),
        compiler_params=PARAMS, cost_estimate=cost(5), name="block",
    )(places, decay_log, segs, gain, incoming, prefix, queries, key_rows, values, *after)


def product_kernel(jobs, inputs, off_ref, *refs):
    rows, weights, outs = refs[:inputs], refs[inputs:inputs + 2], refs[inputs + 2:]
    for (row, side), out in zip(jobs, outs):
        weight = weights[side][...] if len(weights[side].shape) == 2 else weights[side][0]
        out[...] = dot(rows[row][...], weight).astype(out.dtype)


def product_us(jobs, wide):
    return 2.0 + 0.9 * len(jobs) * wide / 512


def product(offsets, jobs, dtypes, rows, weights, after=()):
    size, depth = rows[0].shape
    gathered = len(weights[0].shape) == 3
    if gathered:
        wide = weights[0].shape[2]
        slices = weights[0].shape[0] // 2
        spec = lambda side: pl.BlockSpec((1, depth, wide), lambda j, off: (j * slices + off[side], 0, 0))
        steps = 2
    else:
        wide = 512
        steps = weights[0].shape[1] // wide
        spec = lambda side: pl.BlockSpec((depth, wide), lambda j, off: (0, j))
    return pl.pallas_call(
        ignore(functools.partial(product_kernel, jobs, len(rows)), 3 + len(rows), len(after)),
        grid_spec=pltpu.PrefetchScalarGridSpec(
            num_scalar_prefetch=1,
            grid=(steps,),
            in_specs=[whole((size, depth))] * len(rows) + [spec(0), spec(1)] + anywhere(after),
            out_specs=[pl.BlockSpec((size, wide), lambda j, off: (0, j))] * len(jobs),
        ),
        out_shape=[jax.ShapeDtypeStruct((size, steps * wide), d) for d in dtypes],
        compiler_params=PARAMS, cost_estimate=cost(product_us(jobs, steps * wide)), name="product",
    )(offsets, *rows, *weights, *after)


def plain(shards, queries, key_rows, values, decay_codes, segment_ids, norm_gain, out_weight):
    tokens, width = queries.shape
    me = lax.axis_index("seq")
    decay_log = jnp.log1p(-decay_codes.astype(F32) / 65536.0)
    segs = segment_ids.reshape(-1, SPAN)
    prefix, state = shard_state(decay_log, segs, key_rows, values)
    gathered = lax.all_gather(state, "seq", axis=0)
    incoming = incoming_state(me, tokens, decay_log, segs, width, [gathered[s] for s in range(shards - 1)], range(shards - 1))
    places = jnp.arange(tokens // SPAN).astype(jnp.int32)
    rows = [normed(places, i, decay_log, segs, norm_gain[None], incoming, prefix, queries, key_rows, values)
            for i in range(tokens // SPAN)]
    weight = lax.all_gather(out_weight, "seq", axis=1, tiled=True)
    partials = jnp.dot(jnp.concatenate(rows), weight, preferred_element_type=F32)
    return lax.psum_scatter(partials.astype(BF16), "head", scatter_dimension=0, tiled=True)


def finish_kernel(half, off_ref, left, left_back, left_own, right, right_back, right_own, _, out):
    step = pl.program_id(0)

    @pl.when(step < half)
    def _():
        out[...] = (left[...].astype(F32) + left_back[...].astype(F32) + left_own[...]).astype(out.dtype)

    @pl.when(step >= half)
    def _():
        out[...] = (right[...].astype(F32) + right_back[...].astype(F32) + right_own[...]).astype(out.dtype)


def finish(spots, tile, lefts, rights, out, after=()):
    rows, wide = lefts[0].shape
    half = wide // tile
    early = pl.BlockSpec((rows, tile), lambda j, off: (0, jnp.minimum(j, half - 1)))
    late = pl.BlockSpec((rows, tile), lambda j, off: (0, jnp.maximum(j, half) - half))
    return pl.pallas_call(
        ignore(functools.partial(finish_kernel, half), 8, len(after)),
        grid_spec=pltpu.PrefetchScalarGridSpec(
            num_scalar_prefetch=1,
            grid=(2 * half,),
            in_specs=[early] * 3 + [late] * 3 + [pl.BlockSpec(memory_space=pl.ANY)] + anywhere(after),
            out_specs=pl.BlockSpec((rows, tile), lambda j, off: (0, off[j])),
        ),
        out_shape=jax.ShapeDtypeStruct(out.shape, out.dtype),
        input_output_aliases={7: 0},
        compiler_params=PARAMS, cost_estimate=cost(2), name="finish",
    )(spots, *lefts, *rights, out, *after)


def merge_kernel(a, b, c, d, left, right):
    left[...] = (a[...].astype(F32) + b[...]).astype(BF16)
    right[...] = (c[...].astype(F32) + d[...]).astype(BF16)


def merge(came, own, came_back, own_back, after=()):
    rows, wide = came.shape
    part = pl.BlockSpec((rows, 512), lambda j: (0, j))
    shape = jax.ShapeDtypeStruct(came.shape, BF16)
    return pl.pallas_call(
        ignore(merge_kernel, 4, len(after)),
        grid=(wide // 512,),
        in_specs=[part] * 4 + anywhere(after),
        out_specs=[part] * 2,
        out_shape=[shape, shape],
        compiler_params=PARAMS, cost_estimate=cost(1.5), name="merge",
    )(came, own, came_back, own_back, *after)


def cutting_kernel(off_ref, rows, left, right, x_ref, left_out, right_out, most, rest):
    product_kernel(((0, 0), (0, 1)), 1, off_ref, rows, left, right, left_out, right_out)
    step = pl.program_id(0)

    @pl.when(step < pl.num_programs(0) - 1)
    def _():
        most[...] = x_ref[...]

    @pl.when(step == pl.num_programs(0) - 1)
    def _():
        rest[...] = x_ref[...]


def cutting_product(start, rows, left, right):
    size, depth = rows.shape
    steps = left.shape[1] // 512
    weight = pl.BlockSpec((depth, 512), lambda j, off: (0, j))
    product_out = pl.BlockSpec((size, 512), lambda j, off: (0, j))
    shapes = [(size, left.shape[1])] * 2 + [(depth, 256 * (steps - 1)), (depth, 256)]
    return pl.pallas_call(
        cutting_kernel,
        grid_spec=pltpu.PrefetchScalarGridSpec(
            num_scalar_prefetch=1,
            grid=(steps,),
            in_specs=[whole((size, depth)), weight, weight, pl.BlockSpec((depth, 256), lambda j, off: (0, off[0] + j))],
            out_specs=[product_out] * 2 + [pl.BlockSpec((depth, 256), lambda j, off: (0, jnp.minimum(j, steps - 2))),
                                           pl.BlockSpec((depth, 256), lambda j, off: (0, 0))],
        ),
        out_shape=[jax.ShapeDtypeStruct(x, BF16) for x in shapes],
        compiler_params=PARAMS, cost_estimate=cost(8), name="product",
    )(start, rows, left, right, left)


def ringed(queries, key_rows, values, decay_codes, segment_ids, norm_gain, out_weight):
    tokens, width = queries.shape
    me, line, copy = lax.axis_index("seq"), lax.axis_index("head"), lax.axis_index("grp")
    core, chip = me % 2, me // 2
    ways = [lambda x, d=d: lax.ppermute(x, "head", [(i, (i + d) % 4) for i in range(4)]) for d in (1, 3)]
    sibling = lambda x: lax.ppermute(x, "seq", [(0, 1), (1, 0), (2, 3), (3, 2)])
    onward = lambda x: lax.ppermute(x, "seq", [(0, 2), (1, 3)])
    gather = lambda x: lax.all_gather(x, ("grp", "seq"), axis=0)

    depth, columns = out_weight.shape
    half = columns // 2
    cuts = [(0, half // 3 * 2), (half // 3 * 2, half)]
    decay_log = jnp.log1p(-decay_codes.astype(F32) / 65536.0)
    segs = segment_ids.reshape(-1, SPAN)
    gain = norm_gain[None]
    places = jnp.stack([(line + b) % 4 for b in range(4)]).astype(jnp.int32)
    slices = [chip * 2 + core, chip * 2 + 1 - core, (1 - chip) * 2 + core, (1 - chip) * 2 + 1 - core]
    far_offsets = jnp.stack(slices[2:]).astype(jnp.int32)
    start = (copy * (half // 256)).reshape(1).astype(jnp.int32)

    near = sibling(out_weight)
    prefix, state = shard_state(decay_log, segs, key_rows, values)
    state_x, state_c = onward(state), sibling(state)
    state_d = sibling(state_x)
    owners = [jnp.where(core == 1, me - 1, 4), jnp.where(me >= 2, me - 2, 4), jnp.where(me >= 2, 1 - core, 4)]
    incoming = incoming_state(me, tokens, decay_log, segs, width, [state_c, state_x, state_d], owners)
    norm = lambda i, *after: normed(places, i, decay_log, segs, gain, incoming, prefix, queries, key_rows, values, after=after)

    chunks = [(slices[:2], 512, list(range(columns // 512)))]
    for low, high in cuts:
        chunks.append((slices[2:], 256, [t * (half // 256) + i for t in range(2) for i in range(low // 256, high // 256)]))
    rows = {2: norm(2)}
    out = jnp.zeros((SPAN, 4 * columns), BF16)
    last, waiting = rows[2], None
    for number, (owners, tile, tiles) in enumerate(chunks):
        def mul(jobs, dtypes, *after):
            used = sorted({r for r, _ in jobs})
            where = [(used.index(r), side) for r, side in jobs]
            pair = [out_weight, near] if number < 1 else [far[number - 1]] * 2
            return product(far_offsets, where, dtypes, [rows[r] for r in used], pair, after=after)

        if number == 0:
            *across, most, rest = cutting_product(start, rows[2], out_weight, near)
            far = [gather(x) for x in (most, rest)]
        else:
            across = mul([(2, 0), (2, 1)], [BF16] * 2, last)
        come = [way(x) for way, x in zip(ways, across)]
        if 1 not in rows:
            rows[1] = norm(1, across[1])
            rows[3] = norm(3, rows[1])
        left, right, *mine = mul([(3, 0), (1, 1), (1, 0), (3, 1)], [BF16, BF16, F32, F32], across[0], rows[3])
        straight = [ways[1](left), ways[0](right)]
        if 0 not in rows:
            rows[0] = norm(0, left)
        own = mul([(0, 0), (0, 1)], [F32] * 2, left)
        if waiting is not None:
            out = waiting(out, own[0])
        sums = merge(come[0], mine[0], come[1], mine[1], after=[own[0], out])
        last = sums[0]
        sums = [way(x) for way, x in zip(ways, sums)]
        spots = jnp.stack([owner * (columns // tile) + t for owner in owners for t in tiles]).astype(jnp.int32)

        def waiting(out, after, spots=spots, tile=tile, sums=sums, straight=straight, own=own):
            return finish(spots, tile, [sums[0], straight[0], own[0]], [straight[1], sums[1], own[1]], out, after=[after])

    return waiting(out, last)


def per_device(sizes, *args):
    if sizes == (2, 4, 4) and args[-1].shape[1] == 1536:
        return ringed(*args)
    return plain(sizes[1], *args)


def solution(mesh):
    in_specs = (
        P(("grp", "seq"), "head"),
        P(("grp", "seq"), "head"),
        P(("grp", "seq"), "head"),
        P("head"),
        P(("grp", "seq")),
        P("head"),
        P("head", "seq"),
    )
    out_specs = P(("grp", "seq", "head"), None)
    sizes = (mesh.shape["grp"], mesh.shape["seq"], mesh.shape["head"])
    return jax.shard_map(
        functools.partial(per_device, sizes), mesh=mesh, in_specs=in_specs, out_specs=out_specs, check_vma=False
    )
```

```python
import functools

import jax
import jax.numpy as jnp
from jax import lax
from jax.experimental import pallas as pl
from jax.experimental.pallas import tpu as pltpu
from jax.sharding import PartitionSpec as P

SPAN = 256
HEAD = 128
SEG_ROWS = 16
F32 = jnp.float32
BF16 = jnp.bfloat16
SCALE = 0.02


def cost(us):
    return pl.CostEstimate(flops=int(us * SCALE * 1.1535e9), bytes_accessed=1, transcendentals=0)


PARAMS = pltpu.CompilerParams(vmem_limit_bytes=48 << 20)
ALL_VMEM = pltpu.CompilerParams(vmem_limit_bytes=62 << 20)


def iota(shape, dim):
    return lax.broadcasted_iota(jnp.int32, shape, dim)


def dot(a, b, dims=((1,), (0,))):
    return lax.dot_general(a, b, (dims, ((), ())), preferred_element_type=F32)


def ignore(kernel, inputs, extra):
    if not extra:
        return kernel
    return lambda *refs: kernel(*refs[:inputs], *refs[inputs + extra:])


def anywhere(extra):
    return [pl.BlockSpec(memory_space=pl.ANY)] * len(extra)


def smem():
    return pl.BlockSpec(memory_space=pltpu.SMEM)


def whole(shape):
    return pl.BlockSpec(shape, lambda *i: (0,) * len(shape))


def block_bounds(row, before):
    last = row[:, SPAN - 1:]
    continued = jnp.sum((row == before).astype(jnp.int32))
    start = SPAN - jnp.sum((row == last).astype(jnp.int32))
    return continued, start, jnp.sum((last == before).astype(jnp.int32)), last


def state_kernel(heads_step, decay_ref, row_ref, k_ref, v_ref, prefix_ref, out_ref, bounds):
    step = pl.program_id(0)
    blocks = k_ref.shape[0] // SPAN
    heads = pl.num_programs(0) * heads_step

    @pl.when(step == 0)
    def _():
        before = jnp.full((1, 1), -1, jnp.int32)
        for b in range(blocks):
            _, bounds[0, b], bounds[1, b], before = block_bounds(row_ref[b:b + 1, :], before)
        out_ref[heads * HEAD:, :] = jnp.broadcast_to(before.astype(F32), (SEG_ROWS, HEAD)).astype(BF16)

    place = iota((SPAN, HEAD), 0)
    count = place.astype(F32)
    for j in range(0, heads_step, 2):
        heads_here = [step * heads_step + j + i for i in range(2)]
        pair = slice(j * HEAD, (j + 2) * HEAD)
        rows_out = [pl.ds(pl.multiple_of(head * HEAD, HEAD), HEAD) for head in heads_here]
        tail_decay = jnp.concatenate([jnp.exp((SPAN - 1.0 - count) * decay_ref[head]) for head in heads_here], axis=1)
        block_decay = [jnp.exp(jnp.full((HEAD, HEAD), SPAN, F32) * decay_ref[head]) for head in heads_here]
        memory = [jnp.zeros((HEAD, HEAD), F32)] * 2
        for b in range(blocks):
            rows = slice(b * SPAN, (b + 1) * SPAN)
            started = iota((SPAN, 2 * HEAD), 0) >= bounds[0, b]
            kept = jnp.where(started, k_ref[rows, pair].astype(F32) * tail_decay, 0.0).astype(BF16)
            added = dot(kept, v_ref[rows, pair], ((0,), (0,)))
            for i in range(2):
                prefix_ref[b, rows_out[i], :] = memory[i].astype(BF16)
                own = added[i * HEAD:(i + 1) * HEAD, i * HEAD:(i + 1) * HEAD]
                memory[i] = own + jnp.where(bounds[1, b] > 0, block_decay[i] * memory[i], 0.0)
        for i in range(2):
            out_ref[rows_out[i], :] = memory[i].astype(BF16)


def block_kernel(order, heads_step, block_ref, decay_ref, row_ref, gain_ref, incoming_ref, prefix_ref, q_ref, k_ref, v_ref, out_ref,
                 mask, bounds):
    step = pl.program_id(0)
    block = block_ref[order]

    @pl.when(step == 0)
    def _():
        row = row_ref[pl.ds(block, 1), :]
        earlier = row_ref[pl.ds(jnp.maximum(block - 1, 0), 1), :][:, SPAN - 1:]
        bounds[0], _, _, _ = block_bounds(row, jnp.where(block > 0, earlier, -1))
        bounds[1] = jnp.sum((row == row_ref[0:1, 0:1]).astype(jnp.int32))
        across = jnp.broadcast_to(row, (SPAN, SPAN)).astype(F32)
        same = jnp.logical_and(iota((SPAN, SPAN), 0) >= iota((SPAN, SPAN), 1), across == across.T)
        mask[...] = jnp.where(same, 1.0, 0.0)

    distance = jnp.maximum(iota((SPAN, SPAN), 0) - iota((SPAN, SPAN), 1), 0).astype(F32)
    place = iota((SPAN, HEAD), 0)
    count = (place + 1).astype(F32)
    from_start = count + (block * SPAN).astype(F32)
    for j in range(heads_step):
        decay = decay_ref[step * heads_step + j]
        cols = slice(j * HEAD, (j + 1) * HEAD)
        q, v = q_ref[:, cols], v_ref[:, cols]
        weights = (dot(q, k_ref[:, cols], ((1,), (1,))) * jnp.exp(distance * decay) * mask[...]).astype(BF16)
        both = dot(q, jnp.concatenate([prefix_ref[0, cols, :], incoming_ref[cols, :]], axis=1))
        att = dot(weights, v)
        att = att + jnp.where(place < bounds[0], both[:, :HEAD] * jnp.exp(count * decay), 0.0)
        att = att + jnp.where(place < bounds[1], both[:, HEAD:] * jnp.exp(from_start * decay), 0.0)
        square = jnp.mean(att * att, axis=-1, keepdims=True)
        out_ref[:, cols] = (att * lax.rsqrt(square + 1e-06) * gain_ref[:, cols]).astype(BF16)


def incoming_kernel(me_ref, decay_ref, seg_ref, *refs):
    states, out_ref = refs[:-1], refs[-1]
    me, tokens = me_ref[0], me_ref[1]
    heads = out_ref.shape[0] // HEAD
    first = seg_ref[0:1, 0:1].astype(F32)
    active = []
    for s, ref in enumerate(states):
        seg = ref[heads * HEAD:heads * HEAD + 1, :].astype(F32)
        active.append(jnp.where(jnp.logical_and(seg == first, me_ref[2 + s] < me), 1.0, 0.0))
    for head in range(heads):
        rows = slice(head * HEAD, (head + 1) * HEAD)
        total = jnp.zeros((HEAD, HEAD), F32)
        for s, ref in enumerate(states):
            gap = jnp.maximum(me - 1 - me_ref[2 + s], 0) * tokens
            factor = jnp.exp(jnp.full((1, HEAD), 1.0, F32) * gap.astype(F32) * decay_ref[head]) * active[s]
            total = total + factor * ref[rows, :].astype(F32)
        out_ref[rows, :] = total.astype(BF16)


def chip_kernel(core_ref, decay_ref, own_ref, other_ref, out_ref):
    core, tokens = core_ref[0], core_ref[1]
    width = own_ref.shape[0] - SEG_ROWS
    half = width // 2
    number = slice(width, width + 1)
    own_end, other_end = own_ref[number, :].astype(F32), other_ref[number, :].astype(F32)
    unbroken = own_end == other_end
    out_ref[half:, :] = jnp.broadcast_to(jnp.where(core == 1, own_end, other_end), (SEG_ROWS, HEAD)).astype(BF16)
    span = jnp.full((1, HEAD), 1.0, F32) * tokens.astype(F32)
    for i in range(half // HEAD):
        head = core * (half // HEAD) + i
        rows = pl.ds(pl.multiple_of(head * HEAD, HEAD), HEAD)
        own, other = own_ref[rows, :].astype(F32), other_ref[rows, :].astype(F32)
        first, second = jnp.where(core == 1, other, own), jnp.where(core == 1, own, other)
        carried = jnp.where(unbroken, first * jnp.exp(span * decay_ref[head]), 0.0)
        out_ref[i * HEAD:(i + 1) * HEAD, :] = (second + carried).astype(BF16)


def chip_state(core, tokens, decay_log, own, other):
    vmem = pl.BlockSpec(memory_space=pltpu.VMEM)
    half = (own.shape[0] - SEG_ROWS) // 2
    return pl.pallas_call(
        chip_kernel,
        in_specs=[smem(), smem(), vmem, vmem],
        out_specs=vmem,
        out_shape=jax.ShapeDtypeStruct((half + SEG_ROWS, HEAD), BF16),
        compiler_params=PARAMS, cost_estimate=cost(1), name="chip",
    )(jnp.stack([core, jnp.int32(tokens)]).astype(jnp.int32), decay_log, own, other)


def entering_kernel(place_ref, decay_ref, seg_ref, sibling_ref, direct_ref, passed_ref, out_ref):
    core, chip, tokens = place_ref[0], place_ref[1], place_ref[2]
    width = out_ref.shape[0]
    half = width // 2
    first = seg_ref[0:1, 0:1].astype(F32)
    use_sibling = jnp.logical_and(sibling_ref[width:width + 1, :].astype(F32) == first, core == 1)
    use_chip = jnp.logical_and(direct_ref[half:half + 1, :].astype(F32) == first, chip == 1)
    span = jnp.full((1, HEAD), 1.0, F32) * (core * tokens).astype(F32)
    for head in range(width // HEAD):
        rows = slice(head * HEAD, (head + 1) * HEAD)
        side, there = head * HEAD // half, slice(head * HEAD % half, head * HEAD % half + HEAD)
        before = jnp.where(core == side, direct_ref[there, :], passed_ref[there, :]).astype(F32)
        total = jnp.where(use_chip, before * jnp.exp(span * decay_ref[head]), 0.0)
        total = total + jnp.where(use_sibling, sibling_ref[rows, :].astype(F32), 0.0)
        out_ref[rows, :] = total.astype(BF16)


def entering_state(core, chip, tokens, decay_log, segs, sibling_state, direct, passed_on):
    vmem = pl.BlockSpec(memory_space=pltpu.VMEM)
    return pl.pallas_call(
        entering_kernel,
        in_specs=[smem(), smem()] + [vmem] * 4,
        out_specs=vmem,
        out_shape=jax.ShapeDtypeStruct((sibling_state.shape[0] - SEG_ROWS, HEAD), BF16),
        compiler_params=PARAMS, cost_estimate=cost(1.5), name="entering",
    )(jnp.stack([core, chip, jnp.int32(tokens)]).astype(jnp.int32), decay_log, segs, sibling_state, direct, passed_on)


def shard_state(decay_log, segs, key_rows, values):
    tokens, width = key_rows.shape
    wide = min(8, width // HEAD)
    blocks = tokens // SPAN
    column = pl.BlockSpec((tokens, wide * HEAD), lambda i: (0, i))
    shapes = [(blocks, width, HEAD), (width + SEG_ROWS, HEAD)]
    return pl.pallas_call(
        functools.partial(state_kernel, wide),
        grid=(width // (wide * HEAD),),
        in_specs=[smem(), whole(segs.shape), column, column],
        out_specs=[whole(x) for x in shapes],
        out_shape=[jax.ShapeDtypeStruct(x, BF16) for x in shapes],
        scratch_shapes=[pltpu.SMEM((2, blocks), jnp.int32)],
        compiler_params=PARAMS, cost_estimate=cost(6), name="state",
    )(decay_log, segs, key_rows, values)


def incoming_state(my_index, tokens, decay_log, segs, width, states, owners, after=()):
    numbers = jnp.stack([my_index, jnp.int32(tokens)] + [jnp.int32(0) + o for o in owners]).astype(jnp.int32)
    vmem = pl.BlockSpec(memory_space=pltpu.VMEM)
    return pl.pallas_call(
        ignore(incoming_kernel, 3 + len(states), len(after)),
        in_specs=[smem(), smem()] + [vmem] * (1 + len(states)) + anywhere(after),
        out_specs=vmem,
        out_shape=jax.ShapeDtypeStruct((width, HEAD), BF16),
        compiler_params=PARAMS, cost_estimate=cost(1.5), name="incoming",
    )(numbers, decay_log, segs, *states, *after)


def normed(places, order, decay_log, segs, gain, incoming, prefix, queries, key_rows, values, after=()):
    tokens, width = queries.shape
    wide = min(8, width // HEAD)
    at = pl.BlockSpec((SPAN, wide * HEAD), lambda i, block: (block[order], i))
    states = pl.BlockSpec((wide * HEAD, HEAD), lambda i, block: (i, 0))
    before = pl.BlockSpec((1, wide * HEAD, HEAD), lambda i, block: (block[order], i, 0))
    return pl.pallas_call(
        ignore(functools.partial(block_kernel, order, wide), 9, len(after)),
        grid_spec=pltpu.PrefetchScalarGridSpec(
            num_scalar_prefetch=1,
            grid=(width // (wide * HEAD),),
            in_specs=[smem(), whole(segs.shape), pl.BlockSpec((1, wide * HEAD), lambda i, block: (0, i)), states, before, at, at, at]
            + anywhere(after),
            out_specs=pl.BlockSpec((SPAN, wide * HEAD), lambda i, block: (0, i)),
            scratch_shapes=[pltpu.VMEM((SPAN, SPAN), F32), pltpu.SMEM((2,), jnp.int32)],
        ),
        out_shape=jax.ShapeDtypeStruct((SPAN, width), BF16),
        compiler_params=PARAMS, cost_estimate=cost(5), name="block",
    )(places, decay_log, segs, gain, incoming, prefix, queries, key_rows, values, *after)


def product_kernel(jobs, inputs, off_ref, *refs):
    rows, weights, outs = refs[:inputs], refs[inputs:inputs + 2], refs[inputs + 2:]
    for (row, side), out in zip(jobs, outs):
        weight = weights[side][...] if len(weights[side].shape) == 2 else weights[side][0]
        out[...] = dot(rows[row][...], weight).astype(out.dtype)


def product_us(jobs, wide):
    return 2.0 + 0.9 * len(jobs) * wide / 512


def product(offsets, jobs, dtypes, rows, weights, after=()):
    size, depth = rows[0].shape
    gathered = len(weights[0].shape) == 3
    if gathered:
        wide = weights[0].shape[2]
        slices = weights[0].shape[0] // 2
        spec = lambda side: pl.BlockSpec((1, depth, wide), lambda j, off: (j * slices + off[side], 0, 0))
        steps = 2
    else:
        wide = 512
        steps = weights[0].shape[1] // wide
        spec = lambda side: pl.BlockSpec((depth, wide), lambda j, off: (0, j))
    return pl.pallas_call(
        ignore(functools.partial(product_kernel, jobs, len(rows)), 3 + len(rows), len(after)),
        grid_spec=pltpu.PrefetchScalarGridSpec(
            num_scalar_prefetch=1,
            grid=(steps,),
            in_specs=[whole((size, depth))] * len(rows) + [spec(0), spec(1)] + anywhere(after),
            out_specs=[pl.BlockSpec((size, wide), lambda j, off: (0, j))] * len(jobs),
        ),
        out_shape=[jax.ShapeDtypeStruct((size, steps * wide), d) for d in dtypes],
        compiler_params=PARAMS, cost_estimate=cost(product_us(jobs, steps * wide)), name="product",
    )(offsets, *rows, *weights, *after)


def plain(shards, queries, key_rows, values, decay_codes, segment_ids, norm_gain, out_weight):
    tokens, width = queries.shape
    me = lax.axis_index("seq")
    decay_log = jnp.log1p(-decay_codes.astype(F32) / 65536.0)
    segs = segment_ids.reshape(-1, SPAN)
    prefix, state = shard_state(decay_log, segs, key_rows, values)
    gathered = lax.all_gather(state, "seq", axis=0)
    incoming = incoming_state(me, tokens, decay_log, segs, width, [gathered[s] for s in range(shards - 1)], range(shards - 1))
    places = jnp.arange(tokens // SPAN).astype(jnp.int32)
    rows = [normed(places, i, decay_log, segs, norm_gain[None], incoming, prefix, queries, key_rows, values)
            for i in range(tokens // SPAN)]
    weight = lax.all_gather(out_weight, "seq", axis=1, tiled=True)
    partials = jnp.dot(jnp.concatenate(rows), weight, preferred_element_type=F32)
    return lax.psum_scatter(partials.astype(BF16), "head", scatter_dimension=0, tiled=True)


def finish_kernel(half, off_ref, left, left_back, left_own, right, right_back, right_own, _, out):
    step = pl.program_id(0)

    @pl.when(step < half)
    def _():
        out[...] = (left[...].astype(F32) + left_back[...].astype(F32) + left_own[...]).astype(out.dtype)

    @pl.when(step >= half)
    def _():
        out[...] = (right[...].astype(F32) + right_back[...].astype(F32) + right_own[...]).astype(out.dtype)


def finish(spots, tile, lefts, rights, out, after=()):
    rows, wide = lefts[0].shape
    half = wide // tile
    early = pl.BlockSpec((rows, tile), lambda j, off: (0, jnp.minimum(j, half - 1)))
    late = pl.BlockSpec((rows, tile), lambda j, off: (0, jnp.maximum(j, half) - half))
    return pl.pallas_call(
        ignore(functools.partial(finish_kernel, half), 8, len(after)),
        grid_spec=pltpu.PrefetchScalarGridSpec(
            num_scalar_prefetch=1,
            grid=(2 * half,),
            in_specs=[early] * 3 + [late] * 3 + [pl.BlockSpec(memory_space=pl.ANY)] + anywhere(after),
            out_specs=pl.BlockSpec((rows, tile), lambda j, off: (0, off[j])),
        ),
        out_shape=jax.ShapeDtypeStruct(out.shape, out.dtype),
        input_output_aliases={7: 0},
        compiler_params=PARAMS, cost_estimate=cost(2), name="finish",
    )(spots, *lefts, *rights, out, *after)


def merge_kernel(a, b, c, d, left, right):
    left[...] = (a[...].astype(F32) + b[...]).astype(BF16)
    right[...] = (c[...].astype(F32) + d[...]).astype(BF16)


def merge(came, own, came_back, own_back, after=()):
    rows, wide = came.shape
    part = pl.BlockSpec((rows, 512), lambda j: (0, j))
    shape = jax.ShapeDtypeStruct(came.shape, BF16)
    return pl.pallas_call(
        ignore(merge_kernel, 4, len(after)),
        grid=(wide // 512,),
        in_specs=[part] * 4 + anywhere(after),
        out_specs=[part] * 2,
        out_shape=[shape, shape],
        compiler_params=PARAMS, cost_estimate=cost(1.5), name="merge",
    )(came, own, came_back, own_back, *after)


def cut_kernel(off_ref, x_ref, most, rest):
    step = pl.program_id(0)

    @pl.when(step < pl.num_programs(0) - 1)
    def _():
        most[...] = x_ref[...]

    @pl.when(step == pl.num_programs(0) - 1)
    def _():
        rest[...] = x_ref[...]


def cut(start, wide, weight, after):
    depth = weight.shape[0]
    return pl.pallas_call(
        ignore(cut_kernel, 2, len(after)),
        grid_spec=pltpu.PrefetchScalarGridSpec(
            num_scalar_prefetch=1,
            grid=(wide // 256,),
            in_specs=[pl.BlockSpec((depth, 256), lambda j, off: (0, off[0] + j))] + anywhere(after),
            out_specs=[pl.BlockSpec((depth, 256), lambda j, off: (0, jnp.minimum(j, wide // 256 - 2))),
                       pl.BlockSpec((depth, 256), lambda j, off: (0, 0))],
        ),
        out_shape=[jax.ShapeDtypeStruct((depth, w), weight.dtype) for w in (wide - 256, 256)],
        compiler_params=ALL_VMEM, cost_estimate=cost(4), name="cut",
    )(start, weight, *after)


def held(xs, after):
    n = len(xs)
    return pl.pallas_call(
        lambda *refs: None,
        in_specs=anywhere(xs) + anywhere(after),
        out_specs=anywhere(xs),
        out_shape=[jax.ShapeDtypeStruct(x.shape, x.dtype) for x in xs],
        input_output_aliases={i: i for i in range(n)},
        compiler_params=ALL_VMEM, cost_estimate=cost(1), name="held",
    )(*xs, *after)


def ringed(queries, key_rows, values, decay_codes, segment_ids, norm_gain, out_weight):
    tokens, width = queries.shape
    me, line, copy = lax.axis_index("seq"), lax.axis_index("head"), lax.axis_index("grp")
    core, chip = me % 2, me // 2
    ways = [lambda x, d=d: lax.ppermute(x, "head", [(i, (i + d) % 4) for i in range(4)]) for d in (1, 3)]
    sibling = lambda x: lax.ppermute(x, "seq", [(0, 1), (1, 0), (2, 3), (3, 2)])
    onward = lambda x: lax.ppermute(x, "seq", [(0, 2), (1, 3)])
    gather = lambda x: lax.all_gather(x, ("grp", "seq"), axis=0)

    depth, columns = out_weight.shape
    half = columns // 2
    cuts = [(0, half // 3 * 2), (half // 3 * 2, half)]
    decay_log = jnp.log1p(-decay_codes.astype(F32) / 65536.0)
    segs = segment_ids.reshape(-1, SPAN)
    gain = norm_gain[None]
    places = jnp.stack([(line + b) % 4 for b in range(4)]).astype(jnp.int32)
    slices = [chip * 2 + core, chip * 2 + 1 - core, (1 - chip) * 2 + core, (1 - chip) * 2 + 1 - core]
    far_offsets = jnp.stack(slices[2:]).astype(jnp.int32)
    start = (copy * (half // 256)).reshape(1).astype(jnp.int32)

    near = sibling(out_weight)
    prefix, state = shard_state(decay_log, segs, key_rows, values)
    state_c = sibling(state)
    state_x = onward(chip_state(core, tokens, decay_log, state, state_c))
    far = [gather(x) for x in held(cut(start, half, out_weight, [state_c, near]), [state_x])]
    incoming = entering_state(core, chip, tokens, decay_log, segs, state_c, state_x, sibling(state_x))
    norm = lambda i, *after: normed(places, i, decay_log, segs, gain, incoming, prefix, queries, key_rows, values, after=after)

    chunks = [(slices[:2], 512, list(range(columns // 512)))]
    for low, high in cuts:
        chunks.append((slices[2:], 256, [t * (half // 256) + i for t in range(2) for i in range(low // 256, high // 256)]))
    rows = {2: norm(2)}
    out = jnp.zeros((SPAN, 4 * columns), BF16)
    last, waiting = rows[2], None
    for number, (owners, tile, tiles) in enumerate(chunks):
        def mul(jobs, dtypes, *after):
            used = sorted({r for r, _ in jobs})
            where = [(used.index(r), side) for r, side in jobs]
            pair = [out_weight, near] if number < 1 else [far[number - 1]] * 2
            return product(far_offsets, where, dtypes, [rows[r] for r in used], pair, after=after)

        across = mul([(2, 0), (2, 1)], [BF16] * 2, last)
        come = [way(x) for way, x in zip(ways, across)]
        if 1 not in rows:
            rows[1] = norm(1, across[1])
            rows[3] = norm(3, rows[1])
        left, right, *mine = mul([(3, 0), (1, 1), (1, 0), (3, 1)], [BF16, BF16, F32, F32], across[0], rows[3])
        straight = [ways[1](left), ways[0](right)]
        if 0 not in rows:
            rows[0] = norm(0, left)
        own = mul([(0, 0), (0, 1)], [F32] * 2, left)
        if waiting is not None:
            out = waiting(out, own[0])
        sums = merge(come[0], mine[0], come[1], mine[1], after=[own[0], out])
        last = sums[0]
        sums = [way(x) for way, x in zip(ways, sums)]
        spots = jnp.stack([owner * (columns // tile) + t for owner in owners for t in tiles]).astype(jnp.int32)

        def waiting(out, after, spots=spots, tile=tile, sums=sums, straight=straight, own=own):
            return finish(spots, tile, [sums[0], straight[0], own[0]], [straight[1], sums[1], own[1]], out, after=[after])

    return waiting(out, last)


def per_device(sizes, *args):
    if sizes == (2, 4, 4) and args[-1].shape[1] == 1536:
        return ringed(*args)
    return plain(sizes[1], *args)


def solution(mesh):
    in_specs = (
        P(("grp", "seq"), "head"),
        P(("grp", "seq"), "head"),
        P(("grp", "seq"), "head"),
        P("head"),
        P(("grp", "seq")),
        P("head"),
        P("head", "seq"),
    )
    out_specs = P(("grp", "seq", "head"), None)
    sizes = (mesh.shape["grp"], mesh.shape["seq"], mesh.shape["head"])
    return jax.shard_map(
        functools.partial(per_device, sizes), mesh=mesh, in_specs=in_specs, out_specs=out_specs, check_vma=False
    )
```

```python
import functools

import jax
import jax.numpy as jnp
from jax import lax
from jax.experimental import pallas as pl
from jax.experimental.pallas import tpu as pltpu
from jax.sharding import PartitionSpec as P

SPAN = 256
HEAD = 128
SEG_ROWS = 16
F32 = jnp.float32
BF16 = jnp.bfloat16
SCALE = 0.02


def cost(us):
    return pl.CostEstimate(flops=int(us * SCALE * 1.1535e9), bytes_accessed=1, transcendentals=0)


PARAMS = pltpu.CompilerParams(vmem_limit_bytes=48 << 20)
ALL_VMEM = pltpu.CompilerParams(vmem_limit_bytes=62 << 20)


def iota(shape, dim):
    return lax.broadcasted_iota(jnp.int32, shape, dim)


def dot(a, b, dims=((1,), (0,))):
    return lax.dot_general(a, b, (dims, ((), ())), preferred_element_type=F32)


def ignore(kernel, inputs, extra):
    if not extra:
        return kernel
    return lambda *refs: kernel(*refs[:inputs], *refs[inputs + extra:])


def anywhere(extra):
    return [pl.BlockSpec(memory_space=pl.ANY)] * len(extra)


def smem():
    return pl.BlockSpec(memory_space=pltpu.SMEM)


def whole(shape):
    return pl.BlockSpec(shape, lambda *i: (0,) * len(shape))


def block_bounds(row, before):
    last = row[:, SPAN - 1:]
    continued = jnp.sum((row == before).astype(jnp.int32))
    start = SPAN - jnp.sum((row == last).astype(jnp.int32))
    return continued, start, jnp.sum((last == before).astype(jnp.int32)), last


def state_kernel(heads_step, decay_ref, row_ref, k_ref, v_ref, prefix_ref, out_ref, bounds):
    step = pl.program_id(0)
    blocks = k_ref.shape[0] // SPAN
    heads = pl.num_programs(0) * heads_step

    @pl.when(step == 0)
    def _():
        before = jnp.full((1, 1), -1, jnp.int32)
        for b in range(blocks):
            _, bounds[0, b], bounds[1, b], before = block_bounds(row_ref[b:b + 1, :], before)
        out_ref[heads * HEAD:, :] = jnp.broadcast_to(before.astype(F32), (SEG_ROWS, HEAD)).astype(BF16)

    place = iota((SPAN, HEAD), 0)
    count = place.astype(F32)
    for j in range(0, heads_step, 2):
        heads_here = [step * heads_step + j + i for i in range(2)]
        pair = slice(j * HEAD, (j + 2) * HEAD)
        rows_out = [pl.ds(pl.multiple_of(head * HEAD, HEAD), HEAD) for head in heads_here]
        tail_decay = jnp.concatenate([jnp.exp((SPAN - 1.0 - count) * decay_ref[head]) for head in heads_here], axis=1)
        block_decay = [jnp.exp(jnp.full((HEAD, HEAD), SPAN, F32) * decay_ref[head]) for head in heads_here]
        memory = [jnp.zeros((HEAD, HEAD), F32)] * 2
        for b in range(blocks):
            rows = slice(b * SPAN, (b + 1) * SPAN)
            started = iota((SPAN, 2 * HEAD), 0) >= bounds[0, b]
            kept = jnp.where(started, k_ref[rows, pair].astype(F32) * tail_decay, 0.0).astype(BF16)
            added = dot(kept, v_ref[rows, pair], ((0,), (0,)))
            for i in range(2):
                prefix_ref[b, rows_out[i], :] = memory[i].astype(BF16)
                own = added[i * HEAD:(i + 1) * HEAD, i * HEAD:(i + 1) * HEAD]
                memory[i] = own + jnp.where(bounds[1, b] > 0, block_decay[i] * memory[i], 0.0)
        for i in range(2):
            out_ref[rows_out[i], :] = memory[i].astype(BF16)


def block_kernel(order, heads_step, block_ref, decay_ref, row_ref, gain_ref, incoming_ref, prefix_ref, q_ref, k_ref, v_ref, out_ref,
                 mask, bounds):
    step = pl.program_id(0)
    block = block_ref[order]

    @pl.when(step == 0)
    def _():
        row = row_ref[pl.ds(block, 1), :]
        earlier = row_ref[pl.ds(jnp.maximum(block - 1, 0), 1), :][:, SPAN - 1:]
        bounds[0], _, _, _ = block_bounds(row, jnp.where(block > 0, earlier, -1))
        bounds[1] = jnp.sum((row == row_ref[0:1, 0:1]).astype(jnp.int32))
        across = jnp.broadcast_to(row, (SPAN, SPAN)).astype(F32)
        same = jnp.logical_and(iota((SPAN, SPAN), 0) >= iota((SPAN, SPAN), 1), across == across.T)
        mask[...] = jnp.where(same, 1.0, 0.0)

    distance = jnp.maximum(iota((SPAN, SPAN), 0) - iota((SPAN, SPAN), 1), 0).astype(F32)
    place = iota((SPAN, HEAD), 0)
    count = (place + 1).astype(F32)
    from_start = count + (block * SPAN).astype(F32)
    for j in range(heads_step):
        decay = decay_ref[step * heads_step + j]
        cols = slice(j * HEAD, (j + 1) * HEAD)
        q, v = q_ref[:, cols], v_ref[:, cols]
        weights = (dot(q, k_ref[:, cols], ((1,), (1,))) * jnp.exp(distance * decay) * mask[...]).astype(BF16)
        both = dot(q, jnp.concatenate([prefix_ref[0, cols, :], incoming_ref[cols, :]], axis=1))
        att = dot(weights, v)
        att = att + jnp.where(place < bounds[0], both[:, :HEAD] * jnp.exp(count * decay), 0.0)
        att = att + jnp.where(place < bounds[1], both[:, HEAD:] * jnp.exp(from_start * decay), 0.0)
        square = jnp.mean(att * att, axis=-1, keepdims=True)
        out_ref[:, cols] = (att * lax.rsqrt(square + 1e-06) * gain_ref[:, cols]).astype(BF16)


def incoming_kernel(me_ref, decay_ref, seg_ref, *refs):
    states, out_ref = refs[:-1], refs[-1]
    me, tokens = me_ref[0], me_ref[1]
    heads = out_ref.shape[0] // HEAD
    first = seg_ref[0:1, 0:1].astype(F32)
    active = []
    for s, ref in enumerate(states):
        seg = ref[heads * HEAD:heads * HEAD + 1, :].astype(F32)
        active.append(jnp.where(jnp.logical_and(seg == first, me_ref[2 + s] < me), 1.0, 0.0))
    for head in range(heads):
        rows = slice(head * HEAD, (head + 1) * HEAD)
        total = jnp.zeros((HEAD, HEAD), F32)
        for s, ref in enumerate(states):
            gap = jnp.maximum(me - 1 - me_ref[2 + s], 0) * tokens
            factor = jnp.exp(jnp.full((1, HEAD), 1.0, F32) * gap.astype(F32) * decay_ref[head]) * active[s]
            total = total + factor * ref[rows, :].astype(F32)
        out_ref[rows, :] = total.astype(BF16)


def chip_kernel(core_ref, decay_ref, own_ref, other_ref, out_ref):
    core, tokens = core_ref[0], core_ref[1]
    width = own_ref.shape[0] - SEG_ROWS
    half = width // 2
    number = slice(width, width + 1)
    own_end, other_end = own_ref[number, :].astype(F32), other_ref[number, :].astype(F32)
    unbroken = own_end == other_end
    out_ref[half:, :] = jnp.broadcast_to(jnp.where(core == 1, own_end, other_end), (SEG_ROWS, HEAD)).astype(BF16)
    span = jnp.full((1, HEAD), 1.0, F32) * tokens.astype(F32)
    for i in range(half // HEAD):
        head = core * (half // HEAD) + i
        rows = pl.ds(pl.multiple_of(head * HEAD, HEAD), HEAD)
        own, other = own_ref[rows, :].astype(F32), other_ref[rows, :].astype(F32)
        first, second = jnp.where(core == 1, other, own), jnp.where(core == 1, own, other)
        carried = jnp.where(unbroken, first * jnp.exp(span * decay_ref[head]), 0.0)
        out_ref[i * HEAD:(i + 1) * HEAD, :] = (second + carried).astype(BF16)


def chip_state(core, tokens, decay_log, own, other):
    vmem = pl.BlockSpec(memory_space=pltpu.VMEM)
    half = (own.shape[0] - SEG_ROWS) // 2
    return pl.pallas_call(
        chip_kernel,
        in_specs=[smem(), smem(), vmem, vmem],
        out_specs=vmem,
        out_shape=jax.ShapeDtypeStruct((half + SEG_ROWS, HEAD), BF16),
        compiler_params=PARAMS, cost_estimate=cost(1), name="chip",
    )(jnp.stack([core, jnp.int32(tokens)]).astype(jnp.int32), decay_log, own, other)


def entering_kernel(place_ref, decay_ref, seg_ref, sibling_ref, direct_ref, passed_ref, out_ref):
    core, chip, tokens = place_ref[0], place_ref[1], place_ref[2]
    width = out_ref.shape[0]
    half = width // 2
    first = seg_ref[0:1, 0:1].astype(F32)
    use_sibling = jnp.logical_and(sibling_ref[width:width + 1, :].astype(F32) == first, core == 1)
    use_chip = jnp.logical_and(direct_ref[half:half + 1, :].astype(F32) == first, chip == 1)
    span = jnp.full((1, HEAD), 1.0, F32) * (core * tokens).astype(F32)
    for head in range(width // HEAD):
        rows = slice(head * HEAD, (head + 1) * HEAD)
        side, there = head * HEAD // half, slice(head * HEAD % half, head * HEAD % half + HEAD)
        before = jnp.where(core == side, direct_ref[there, :], passed_ref[there, :]).astype(F32)
        total = jnp.where(use_chip, before * jnp.exp(span * decay_ref[head]), 0.0)
        total = total + jnp.where(use_sibling, sibling_ref[rows, :].astype(F32), 0.0)
        out_ref[rows, :] = total.astype(BF16)


def entering_state(core, chip, tokens, decay_log, segs, sibling_state, direct, passed_on):
    vmem = pl.BlockSpec(memory_space=pltpu.VMEM)
    return pl.pallas_call(
        entering_kernel,
        in_specs=[smem(), smem()] + [vmem] * 4,
        out_specs=vmem,
        out_shape=jax.ShapeDtypeStruct((sibling_state.shape[0] - SEG_ROWS, HEAD), BF16),
        compiler_params=PARAMS, cost_estimate=cost(1.5), name="entering",
    )(jnp.stack([core, chip, jnp.int32(tokens)]).astype(jnp.int32), decay_log, segs, sibling_state, direct, passed_on)


def shard_state(decay_log, segs, key_rows, values):
    tokens, width = key_rows.shape
    wide = min(8, width // HEAD)
    blocks = tokens // SPAN
    column = pl.BlockSpec((tokens, wide * HEAD), lambda i: (0, i))
    shapes = [(blocks, width, HEAD), (width + SEG_ROWS, HEAD)]
    return pl.pallas_call(
        functools.partial(state_kernel, wide),
        grid=(width // (wide * HEAD),),
        in_specs=[smem(), whole(segs.shape), column, column],
        out_specs=[whole(x) for x in shapes],
        out_shape=[jax.ShapeDtypeStruct(x, BF16) for x in shapes],
        scratch_shapes=[pltpu.SMEM((2, blocks), jnp.int32)],
        compiler_params=PARAMS, cost_estimate=cost(6), name="state",
    )(decay_log, segs, key_rows, values)


def incoming_state(my_index, tokens, decay_log, segs, width, states, owners, after=()):
    numbers = jnp.stack([my_index, jnp.int32(tokens)] + [jnp.int32(0) + o for o in owners]).astype(jnp.int32)
    vmem = pl.BlockSpec(memory_space=pltpu.VMEM)
    return pl.pallas_call(
        ignore(incoming_kernel, 3 + len(states), len(after)),
        in_specs=[smem(), smem()] + [vmem] * (1 + len(states)) + anywhere(after),
        out_specs=vmem,
        out_shape=jax.ShapeDtypeStruct((width, HEAD), BF16),
        compiler_params=PARAMS, cost_estimate=cost(1.5), name="incoming",
    )(numbers, decay_log, segs, *states, *after)


def normed(places, order, decay_log, segs, gain, incoming, prefix, queries, key_rows, values, after=()):
    tokens, width = queries.shape
    wide = min(8, width // HEAD)
    at = pl.BlockSpec((SPAN, wide * HEAD), lambda i, block: (block[order], i))
    states = pl.BlockSpec((wide * HEAD, HEAD), lambda i, block: (i, 0))
    before = pl.BlockSpec((1, wide * HEAD, HEAD), lambda i, block: (block[order], i, 0))
    return pl.pallas_call(
        ignore(functools.partial(block_kernel, order, wide), 9, len(after)),
        grid_spec=pltpu.PrefetchScalarGridSpec(
            num_scalar_prefetch=1,
            grid=(width // (wide * HEAD),),
            in_specs=[smem(), whole(segs.shape), pl.BlockSpec((1, wide * HEAD), lambda i, block: (0, i)), states, before, at, at, at]
            + anywhere(after),
            out_specs=pl.BlockSpec((SPAN, wide * HEAD), lambda i, block: (0, i)),
            scratch_shapes=[pltpu.VMEM((SPAN, SPAN), F32), pltpu.SMEM((2,), jnp.int32)],
        ),
        out_shape=jax.ShapeDtypeStruct((SPAN, width), BF16),
        compiler_params=PARAMS, cost_estimate=cost(5), name="block",
    )(places, decay_log, segs, gain, incoming, prefix, queries, key_rows, values, *after)


def product_kernel(jobs, inputs, off_ref, *refs):
    rows, weights, outs = refs[:inputs], refs[inputs:inputs + 2], refs[inputs + 2:]
    for (row, side), out in zip(jobs, outs):
        weight = weights[side][...] if len(weights[side].shape) == 2 else weights[side][0]
        out[...] = dot(rows[row][...], weight).astype(out.dtype)


def product_us(jobs, wide):
    return 2.0 + 0.9 * len(jobs) * wide / 512


def product(offsets, jobs, dtypes, rows, weights, after=()):
    size, depth = rows[0].shape
    gathered = len(weights[0].shape) == 3
    if gathered:
        wide = weights[0].shape[2]
        slices = weights[0].shape[0] // 2
        spec = lambda side: pl.BlockSpec((1, depth, wide), lambda j, off: (j * slices + off[side], 0, 0))
        steps = 2
    else:
        wide = 512
        steps = weights[0].shape[1] // wide
        spec = lambda side: pl.BlockSpec((depth, wide), lambda j, off: (0, j))
    return pl.pallas_call(
        ignore(functools.partial(product_kernel, jobs, len(rows)), 3 + len(rows), len(after)),
        grid_spec=pltpu.PrefetchScalarGridSpec(
            num_scalar_prefetch=1,
            grid=(steps,),
            in_specs=[whole((size, depth))] * len(rows) + [spec(0), spec(1)] + anywhere(after),
            out_specs=[pl.BlockSpec((size, wide), lambda j, off: (0, j))] * len(jobs),
        ),
        out_shape=[jax.ShapeDtypeStruct((size, steps * wide), d) for d in dtypes],
        compiler_params=PARAMS, cost_estimate=cost(product_us(jobs, steps * wide)), name="product",
    )(offsets, *rows, *weights, *after)


def plain(shards, queries, key_rows, values, decay_codes, segment_ids, norm_gain, out_weight):
    tokens, width = queries.shape
    me = lax.axis_index("seq")
    decay_log = jnp.log1p(-decay_codes.astype(F32) / 65536.0)
    segs = segment_ids.reshape(-1, SPAN)
    prefix, state = shard_state(decay_log, segs, key_rows, values)
    gathered = lax.all_gather(state, "seq", axis=0)
    incoming = incoming_state(me, tokens, decay_log, segs, width, [gathered[s] for s in range(shards - 1)], range(shards - 1))
    places = jnp.arange(tokens // SPAN).astype(jnp.int32)
    rows = [normed(places, i, decay_log, segs, norm_gain[None], incoming, prefix, queries, key_rows, values)
            for i in range(tokens // SPAN)]
    weight = lax.all_gather(out_weight, "seq", axis=1, tiled=True)
    partials = jnp.dot(jnp.concatenate(rows), weight, preferred_element_type=F32)
    return lax.psum_scatter(partials.astype(BF16), "head", scatter_dimension=0, tiled=True)


def finish_kernel(half, off_ref, left, left_back, left_own, right, right_back, right_own, _, out):
    step = pl.program_id(0)

    @pl.when(step < half)
    def _():
        out[...] = (left[...].astype(F32) + left_back[...].astype(F32) + left_own[...]).astype(out.dtype)

    @pl.when(step >= half)
    def _():
        out[...] = (right[...].astype(F32) + right_back[...].astype(F32) + right_own[...]).astype(out.dtype)


def finish(spots, tile, lefts, rights, out, after=()):
    rows, wide = lefts[0].shape
    half = wide // tile
    early = pl.BlockSpec((rows, tile), lambda j, off: (0, jnp.minimum(j, half - 1)))
    late = pl.BlockSpec((rows, tile), lambda j, off: (0, jnp.maximum(j, half) - half))
    return pl.pallas_call(
        ignore(functools.partial(finish_kernel, half), 8, len(after)),
        grid_spec=pltpu.PrefetchScalarGridSpec(
            num_scalar_prefetch=1,
            grid=(2 * half,),
            in_specs=[early] * 3 + [late] * 3 + [pl.BlockSpec(memory_space=pl.ANY)] + anywhere(after),
            out_specs=pl.BlockSpec((rows, tile), lambda j, off: (0, off[j])),
        ),
        out_shape=jax.ShapeDtypeStruct(out.shape, out.dtype),
        input_output_aliases={7: 0},
        compiler_params=PARAMS, cost_estimate=cost(2), name="finish",
    )(spots, *lefts, *rights, out, *after)


def last_finish_kernel(tile, off_ref, left, left_back, left_own, right, right_back, right_own, _, out, sums, done):
    half = sums.shape[2] // tile
    copies = []
    for side, parts in enumerate(((left, left_back, left_own), (right, right_back, right_own))):
        sums[side] = sum(x[...].astype(F32) for x in parts).astype(sums.dtype)
        for t in range(half):
            place = pl.multiple_of(off_ref[side * half + t] * tile, tile)
            n = side * half + t
            copies.append(pltpu.make_async_copy(sums.at[side, :, pl.ds(t * tile, tile)], out.at[:, pl.ds(place, tile)], done.at[n]))
            copies[-1].start()
    for copy in copies:
        copy.wait()


def last_finish(spots, tile, lefts, rights, out):
    rows, wide = lefts[0].shape
    vmem, any_place = pl.BlockSpec(memory_space=pltpu.VMEM), pl.BlockSpec(memory_space=pl.ANY)
    return pl.pallas_call(
        functools.partial(last_finish_kernel, tile),
        in_specs=[smem()] + [vmem] * 6 + [any_place],
        out_specs=any_place,
        out_shape=jax.ShapeDtypeStruct(out.shape, out.dtype),
        scratch_shapes=[pltpu.VMEM((2, rows, wide), out.dtype), pltpu.SemaphoreType.DMA((2 * wide // tile,))],
        input_output_aliases={7: 0},
        compiler_params=PARAMS, cost_estimate=cost(2), name="finish",
    )(spots, *lefts, *rights, out)


def merge_kernel(a, b, c, d, left, right):
    left[...] = (a[...].astype(F32) + b[...]).astype(BF16)
    right[...] = (c[...].astype(F32) + d[...]).astype(BF16)


def merge(came, own, came_back, own_back, after=()):
    rows, wide = came.shape
    part = pl.BlockSpec((rows, 512), lambda j: (0, j))
    shape = jax.ShapeDtypeStruct(came.shape, BF16)
    return pl.pallas_call(
        ignore(merge_kernel, 4, len(after)),
        grid=(wide // 512,),
        in_specs=[part] * 4 + anywhere(after),
        out_specs=[part] * 2,
        out_shape=[shape, shape],
        compiler_params=PARAMS, cost_estimate=cost(1.5), name="merge",
    )(came, own, came_back, own_back, *after)


def cut_kernel(off_ref, x_ref, most, rest):
    step = pl.program_id(0)

    @pl.when(step < pl.num_programs(0) - 1)
    def _():
        most[...] = x_ref[...]

    @pl.when(step == pl.num_programs(0) - 1)
    def _():
        rest[...] = x_ref[...]


def cut(start, wide, weight, after):
    depth = weight.shape[0]
    return pl.pallas_call(
        ignore(cut_kernel, 2, len(after)),
        grid_spec=pltpu.PrefetchScalarGridSpec(
            num_scalar_prefetch=1,
            grid=(wide // 256,),
            in_specs=[pl.BlockSpec((depth, 256), lambda j, off: (0, off[0] + j))] + anywhere(after),
            out_specs=[pl.BlockSpec((depth, 256), lambda j, off: (0, jnp.minimum(j, wide // 256 - 2))),
                       pl.BlockSpec((depth, 256), lambda j, off: (0, 0))],
        ),
        out_shape=[jax.ShapeDtypeStruct((depth, w), weight.dtype) for w in (wide - 256, 256)],
        compiler_params=ALL_VMEM, cost_estimate=cost(4), name="cut",
    )(start, weight, *after)


def held(xs, after):
    n = len(xs)
    return pl.pallas_call(
        lambda *refs: None,
        in_specs=anywhere(xs) + anywhere(after),
        out_specs=anywhere(xs),
        out_shape=[jax.ShapeDtypeStruct(x.shape, x.dtype) for x in xs],
        input_output_aliases={i: i for i in range(n)},
        compiler_params=ALL_VMEM, cost_estimate=cost(1), name="held",
    )(*xs, *after)


def ringed(queries, key_rows, values, decay_codes, segment_ids, norm_gain, out_weight):
    tokens, width = queries.shape
    me, line, copy = lax.axis_index("seq"), lax.axis_index("head"), lax.axis_index("grp")
    core, chip = me % 2, me // 2
    ways = [lambda x, d=d: lax.ppermute(x, "head", [(i, (i + d) % 4) for i in range(4)]) for d in (1, 3)]
    sibling = lambda x: lax.ppermute(x, "seq", [(0, 1), (1, 0), (2, 3), (3, 2)])
    onward = lambda x: lax.ppermute(x, "seq", [(0, 2), (1, 3)])
    gather = lambda x: lax.all_gather(x, ("grp", "seq"), axis=0)

    depth, columns = out_weight.shape
    half = columns // 2
    cuts = [(0, half // 3 * 2), (half // 3 * 2, half)]
    decay_log = jnp.log1p(-decay_codes.astype(F32) / 65536.0)
    segs = segment_ids.reshape(-1, SPAN)
    gain = norm_gain[None]
    places = jnp.stack([(line + b) % 4 for b in range(4)]).astype(jnp.int32)
    slices = [chip * 2 + core, chip * 2 + 1 - core, (1 - chip) * 2 + core, (1 - chip) * 2 + 1 - core]
    far_offsets = jnp.stack(slices[2:]).astype(jnp.int32)
    start = (copy * (half // 256)).reshape(1).astype(jnp.int32)

    near = sibling(out_weight)
    prefix, state = shard_state(decay_log, segs, key_rows, values)
    state_c = sibling(state)
    state_x = onward(chip_state(core, tokens, decay_log, state, state_c))
    far = [gather(x) for x in held(cut(start, half, out_weight, [state_c, near]), [state_x])]
    incoming = entering_state(core, chip, tokens, decay_log, segs, state_c, state_x, sibling(state_x))
    norm = lambda i, *after: normed(places, i, decay_log, segs, gain, incoming, prefix, queries, key_rows, values, after=after)

    chunks = [(slices[:2], 512, list(range(columns // 512)))]
    for low, high in cuts:
        chunks.append((slices[2:], 256, [t * (half // 256) + i for t in range(2) for i in range(low // 256, high // 256)]))
    rows = {2: norm(2)}
    out = jnp.zeros((SPAN, 4 * columns), BF16)
    last, waiting = rows[2], None
    for number, (owners, tile, tiles) in enumerate(chunks):
        def mul(jobs, dtypes, *after):
            used = sorted({r for r, _ in jobs})
            where = [(used.index(r), side) for r, side in jobs]
            pair = [out_weight, near] if number < 1 else [far[number - 1]] * 2
            return product(far_offsets, where, dtypes, [rows[r] for r in used], pair, after=after)

        across = mul([(2, 0), (2, 1)], [BF16] * 2, last)
        come = [way(x) for way, x in zip(ways, across)]
        if 1 not in rows:
            rows[1] = norm(1, across[1])
            rows[3] = norm(3, rows[1])
        left, right, *mine = mul([(3, 0), (1, 1), (1, 0), (3, 1)], [BF16, BF16, F32, F32], across[0], rows[3])
        straight = [ways[1](left), ways[0](right)]
        if 0 not in rows:
            rows[0] = norm(0, left)
        own = mul([(0, 0), (0, 1)], [F32] * 2, left)
        if waiting is not None:
            out = waiting(out, own[0])
        sums = merge(come[0], mine[0], come[1], mine[1], after=[own[0], out])
        last = sums[0]
        sums = [way(x) for way, x in zip(ways, sums)]
        spots = jnp.stack([owner * (columns // tile) + t for owner in owners for t in tiles]).astype(jnp.int32)

        def waiting(out, after, spots=spots, tile=tile, sums=sums, straight=straight, own=own):
            return finish(spots, tile, [sums[0], straight[0], own[0]], [straight[1], sums[1], own[1]], out, after=[after])

    return last_finish(spots, tile, [sums[0], straight[0], own[0]], [straight[1], sums[1], own[1]], out)


def per_device(sizes, *args):
    if sizes == (2, 4, 4) and args[-1].shape[1] == 1536:
        return ringed(*args)
    return plain(sizes[1], *args)


def solution(mesh):
    in_specs = (
        P(("grp", "seq"), "head"),
        P(("grp", "seq"), "head"),
        P(("grp", "seq"), "head"),
        P("head"),
        P(("grp", "seq")),
        P("head"),
        P("head", "seq"),
    )
    out_specs = P(("grp", "seq", "head"), None)
    sizes = (mesh.shape["grp"], mesh.shape["seq"], mesh.shape["head"])
    return jax.shard_map(
        functools.partial(per_device, sizes), mesh=mesh, in_specs=in_specs, out_specs=out_specs, check_vma=False
    )
```

```python
import functools

import jax
import jax.numpy as jnp
from jax import lax
from jax.experimental import pallas as pl
from jax.experimental.pallas import tpu as pltpu
from jax.sharding import PartitionSpec as P

SPAN = 256
HEAD = 128
SEG_ROWS = 16
F32 = jnp.float32
BF16 = jnp.bfloat16
SCALE = 0.02


def cost(us):
    return pl.CostEstimate(flops=int(us * SCALE * 1.1535e9), bytes_accessed=1, transcendentals=0)


PARAMS = pltpu.CompilerParams(vmem_limit_bytes=48 << 20)
ALL_VMEM = pltpu.CompilerParams(vmem_limit_bytes=62 << 20)


def iota(shape, dim):
    return lax.broadcasted_iota(jnp.int32, shape, dim)


def dot(a, b, dims=((1,), (0,))):
    return lax.dot_general(a, b, (dims, ((), ())), preferred_element_type=F32)


def ignore(kernel, inputs, extra):
    if not extra:
        return kernel
    return lambda *refs: kernel(*refs[:inputs], *refs[inputs + extra:])


def anywhere(extra):
    return [pl.BlockSpec(memory_space=pl.ANY)] * len(extra)


def smem():
    return pl.BlockSpec(memory_space=pltpu.SMEM)


def whole(shape):
    return pl.BlockSpec(shape, lambda *i: (0,) * len(shape))


def block_bounds(row, before):
    last = row[:, SPAN - 1:]
    continued = jnp.sum((row == before).astype(jnp.int32))
    start = SPAN - jnp.sum((row == last).astype(jnp.int32))
    return continued, start, jnp.sum((last == before).astype(jnp.int32)), last


def state_kernel(heads_step, decay_ref, row_ref, k_ref, v_ref, prefix_ref, out_ref, bounds):
    step = pl.program_id(0)
    blocks = k_ref.shape[0] // SPAN
    heads = pl.num_programs(0) * heads_step

    @pl.when(step == 0)
    def _():
        before = jnp.full((1, 1), -1, jnp.int32)
        for b in range(blocks):
            _, bounds[0, b], bounds[1, b], before = block_bounds(row_ref[b:b + 1, :], before)
        out_ref[heads * HEAD:, :] = jnp.broadcast_to(before.astype(F32), (SEG_ROWS, HEAD)).astype(BF16)

    place = iota((SPAN, HEAD), 0)
    count = place.astype(F32)
    for j in range(0, heads_step, 2):
        heads_here = [step * heads_step + j + i for i in range(2)]
        pair = slice(j * HEAD, (j + 2) * HEAD)
        rows_out = [pl.ds(pl.multiple_of(head * HEAD, HEAD), HEAD) for head in heads_here]
        tail_decay = jnp.concatenate([jnp.exp((SPAN - 1.0 - count) * decay_ref[head]) for head in heads_here], axis=1)
        block_decay = [jnp.exp(jnp.full((HEAD, HEAD), SPAN, F32) * decay_ref[head]) for head in heads_here]
        memory = [jnp.zeros((HEAD, HEAD), F32)] * 2
        for b in range(blocks):
            rows = slice(b * SPAN, (b + 1) * SPAN)
            started = iota((SPAN, 2 * HEAD), 0) >= bounds[0, b]
            kept = jnp.where(started, k_ref[rows, pair].astype(F32) * tail_decay, 0.0).astype(BF16)
            added = dot(kept, v_ref[rows, pair], ((0,), (0,)))
            for i in range(2):
                prefix_ref[b, rows_out[i], :] = memory[i].astype(BF16)
                own = added[i * HEAD:(i + 1) * HEAD, i * HEAD:(i + 1) * HEAD]
                memory[i] = own + jnp.where(bounds[1, b] > 0, block_decay[i] * memory[i], 0.0)
        for i in range(2):
            out_ref[rows_out[i], :] = memory[i].astype(BF16)


def block_kernel(order, heads_step, block_ref, decay_ref, row_ref, gain_ref, incoming_ref, prefix_ref, q_ref, k_ref, v_ref, out_ref,
                 mask, bounds):
    step = pl.program_id(0)
    block = block_ref[order]

    @pl.when(step == 0)
    def _():
        row = row_ref[pl.ds(block, 1), :]
        earlier = row_ref[pl.ds(jnp.maximum(block - 1, 0), 1), :][:, SPAN - 1:]
        bounds[0], _, _, _ = block_bounds(row, jnp.where(block > 0, earlier, -1))
        bounds[1] = jnp.sum((row == row_ref[0:1, 0:1]).astype(jnp.int32))
        across = jnp.broadcast_to(row, (SPAN, SPAN)).astype(F32)
        same = jnp.logical_and(iota((SPAN, SPAN), 0) >= iota((SPAN, SPAN), 1), across == across.T)
        mask[...] = jnp.where(same, 1.0, 0.0)

    distance = jnp.maximum(iota((SPAN, SPAN), 0) - iota((SPAN, SPAN), 1), 0).astype(F32)
    place = iota((SPAN, HEAD), 0)
    count = (place + 1).astype(F32)
    from_start = count + (block * SPAN).astype(F32)
    for j in range(heads_step):
        decay = decay_ref[step * heads_step + j]
        cols = slice(j * HEAD, (j + 1) * HEAD)
        q, v = q_ref[:, cols], v_ref[:, cols]
        weights = (dot(q, k_ref[:, cols], ((1,), (1,))) * jnp.exp(distance * decay) * mask[...]).astype(BF16)
        both = dot(q, jnp.concatenate([prefix_ref[0, cols, :], incoming_ref[cols, :]], axis=1))
        att = dot(weights, v)
        att = att + jnp.where(place < bounds[0], both[:, :HEAD] * jnp.exp(count * decay), 0.0)
        att = att + jnp.where(place < bounds[1], both[:, HEAD:] * jnp.exp(from_start * decay), 0.0)
        square = jnp.mean(att * att, axis=-1, keepdims=True)
        out_ref[:, cols] = (att * lax.rsqrt(square + 1e-06) * gain_ref[:, cols]).astype(BF16)


def incoming_kernel(me_ref, decay_ref, seg_ref, *refs):
    states, out_ref = refs[:-1], refs[-1]
    me, tokens = me_ref[0], me_ref[1]
    heads = out_ref.shape[0] // HEAD
    first = seg_ref[0:1, 0:1].astype(F32)
    active = []
    for s, ref in enumerate(states):
        seg = ref[heads * HEAD:heads * HEAD + 1, :].astype(F32)
        active.append(jnp.where(jnp.logical_and(seg == first, me_ref[2 + s] < me), 1.0, 0.0))
    for head in range(heads):
        rows = slice(head * HEAD, (head + 1) * HEAD)
        total = jnp.zeros((HEAD, HEAD), F32)
        for s, ref in enumerate(states):
            gap = jnp.maximum(me - 1 - me_ref[2 + s], 0) * tokens
            factor = jnp.exp(jnp.full((1, HEAD), 1.0, F32) * gap.astype(F32) * decay_ref[head]) * active[s]
            total = total + factor * ref[rows, :].astype(F32)
        out_ref[rows, :] = total.astype(BF16)


def chip_kernel(core_ref, decay_ref, own_ref, other_ref, out_ref):
    core, tokens = core_ref[0], core_ref[1]
    width = own_ref.shape[0] - SEG_ROWS
    half = width // 2
    number = slice(width, width + 1)
    own_end, other_end = own_ref[number, :].astype(F32), other_ref[number, :].astype(F32)
    unbroken = own_end == other_end
    out_ref[half:, :] = jnp.broadcast_to(jnp.where(core == 1, own_end, other_end), (SEG_ROWS, HEAD)).astype(BF16)
    span = jnp.full((1, HEAD), 1.0, F32) * tokens.astype(F32)
    for i in range(half // HEAD):
        head = core * (half // HEAD) + i
        rows = pl.ds(pl.multiple_of(head * HEAD, HEAD), HEAD)
        own, other = own_ref[rows, :].astype(F32), other_ref[rows, :].astype(F32)
        first, second = jnp.where(core == 1, other, own), jnp.where(core == 1, own, other)
        carried = jnp.where(unbroken, first * jnp.exp(span * decay_ref[head]), 0.0)
        out_ref[i * HEAD:(i + 1) * HEAD, :] = (second + carried).astype(BF16)


def chip_state(core, tokens, decay_log, own, other):
    vmem = pl.BlockSpec(memory_space=pltpu.VMEM)
    half = (own.shape[0] - SEG_ROWS) // 2
    return pl.pallas_call(
        chip_kernel,
        in_specs=[smem(), smem(), vmem, vmem],
        out_specs=vmem,
        out_shape=jax.ShapeDtypeStruct((half + SEG_ROWS, HEAD), BF16),
        compiler_params=PARAMS, cost_estimate=cost(1), name="chip",
    )(jnp.stack([core, jnp.int32(tokens)]).astype(jnp.int32), decay_log, own, other)


def entering_kernel(place_ref, decay_ref, seg_ref, sibling_ref, direct_ref, passed_ref, out_ref):
    core, chip, tokens = place_ref[0], place_ref[1], place_ref[2]
    width = out_ref.shape[0]
    half = width // 2
    first = seg_ref[0:1, 0:1].astype(F32)
    use_sibling = jnp.logical_and(sibling_ref[width:width + 1, :].astype(F32) == first, core == 1)
    use_chip = jnp.logical_and(direct_ref[half:half + 1, :].astype(F32) == first, chip == 1)
    span = jnp.full((1, HEAD), 1.0, F32) * (core * tokens).astype(F32)
    for head in range(width // HEAD):
        rows = slice(head * HEAD, (head + 1) * HEAD)
        side, there = head * HEAD // half, slice(head * HEAD % half, head * HEAD % half + HEAD)
        before = jnp.where(core == side, direct_ref[there, :], passed_ref[there, :]).astype(F32)
        total = jnp.where(use_chip, before * jnp.exp(span * decay_ref[head]), 0.0)
        total = total + jnp.where(use_sibling, sibling_ref[rows, :].astype(F32), 0.0)
        out_ref[rows, :] = total.astype(BF16)


def entering_state(core, chip, tokens, decay_log, segs, sibling_state, direct, passed_on):
    vmem = pl.BlockSpec(memory_space=pltpu.VMEM)
    return pl.pallas_call(
        entering_kernel,
        in_specs=[smem(), smem()] + [vmem] * 4,
        out_specs=vmem,
        out_shape=jax.ShapeDtypeStruct((sibling_state.shape[0] - SEG_ROWS, HEAD), BF16),
        compiler_params=PARAMS, cost_estimate=cost(1.5), name="entering",
    )(jnp.stack([core, chip, jnp.int32(tokens)]).astype(jnp.int32), decay_log, segs, sibling_state, direct, passed_on)


def shard_state(decay_log, segs, key_rows, values):
    tokens, width = key_rows.shape
    wide = min(8, width // HEAD)
    blocks = tokens // SPAN
    column = pl.BlockSpec((tokens, wide * HEAD), lambda i: (0, i))
    shapes = [(blocks, width, HEAD), (width + SEG_ROWS, HEAD)]
    return pl.pallas_call(
        functools.partial(state_kernel, wide),
        grid=(width // (wide * HEAD),),
        in_specs=[smem(), whole(segs.shape), column, column],
        out_specs=[whole(x) for x in shapes],
        out_shape=[jax.ShapeDtypeStruct(x, BF16) for x in shapes],
        scratch_shapes=[pltpu.SMEM((2, blocks), jnp.int32)],
        compiler_params=PARAMS, cost_estimate=cost(6), name="state",
    )(decay_log, segs, key_rows, values)


def incoming_state(my_index, tokens, decay_log, segs, width, states, owners, after=()):
    numbers = jnp.stack([my_index, jnp.int32(tokens)] + [jnp.int32(0) + o for o in owners]).astype(jnp.int32)
    vmem = pl.BlockSpec(memory_space=pltpu.VMEM)
    return pl.pallas_call(
        ignore(incoming_kernel, 3 + len(states), len(after)),
        in_specs=[smem(), smem()] + [vmem] * (1 + len(states)) + anywhere(after),
        out_specs=vmem,
        out_shape=jax.ShapeDtypeStruct((width, HEAD), BF16),
        compiler_params=PARAMS, cost_estimate=cost(1.5), name="incoming",
    )(numbers, decay_log, segs, *states, *after)


def normed(places, order, decay_log, segs, gain, incoming, prefix, queries, key_rows, values, after=()):
    tokens, width = queries.shape
    wide = min(8, width // HEAD)
    at = pl.BlockSpec((SPAN, wide * HEAD), lambda i, block: (block[order], i))
    states = pl.BlockSpec((wide * HEAD, HEAD), lambda i, block: (i, 0))
    before = pl.BlockSpec((1, wide * HEAD, HEAD), lambda i, block: (block[order], i, 0))
    return pl.pallas_call(
        ignore(functools.partial(block_kernel, order, wide), 9, len(after)),
        grid_spec=pltpu.PrefetchScalarGridSpec(
            num_scalar_prefetch=1,
            grid=(width // (wide * HEAD),),
            in_specs=[smem(), whole(segs.shape), pl.BlockSpec((1, wide * HEAD), lambda i, block: (0, i)), states, before, at, at, at]
            + anywhere(after),
            out_specs=pl.BlockSpec((SPAN, wide * HEAD), lambda i, block: (0, i)),
            scratch_shapes=[pltpu.VMEM((SPAN, SPAN), F32), pltpu.SMEM((2,), jnp.int32)],
        ),
        out_shape=jax.ShapeDtypeStruct((SPAN, width), BF16),
        compiler_params=PARAMS, cost_estimate=cost(5), name="block",
    )(places, decay_log, segs, gain, incoming, prefix, queries, key_rows, values, *after)


def product_kernel(jobs, inputs, off_ref, *refs):
    rows, weights, outs = refs[:inputs], refs[inputs:inputs + 2], refs[inputs + 2:]
    for (row, side), out in zip(jobs, outs):
        weight = weights[side][...] if len(weights[side].shape) == 2 else weights[side][0]
        out[...] = dot(rows[row][...], weight).astype(out.dtype)


def product_us(jobs, wide):
    return 2.0 + 0.9 * len(jobs) * wide / 512


def product(offsets, jobs, dtypes, rows, weights, after=()):
    size, depth = rows[0].shape
    gathered = len(weights[0].shape) == 3
    if gathered:
        wide = weights[0].shape[2]
        slices = weights[0].shape[0] // 2
        spec = lambda side: pl.BlockSpec((1, depth, wide), lambda j, off: (j * slices + off[side], 0, 0))
        steps = 2
    else:
        wide = 512
        steps = weights[0].shape[1] // wide
        spec = lambda side: pl.BlockSpec((depth, wide), lambda j, off: (0, j))
    return pl.pallas_call(
        ignore(functools.partial(product_kernel, jobs, len(rows)), 3 + len(rows), len(after)),
        grid_spec=pltpu.PrefetchScalarGridSpec(
            num_scalar_prefetch=1,
            grid=(steps,),
            in_specs=[whole((size, depth))] * len(rows) + [spec(0), spec(1)] + anywhere(after),
            out_specs=[pl.BlockSpec((size, wide), lambda j, off: (0, j))] * len(jobs),
        ),
        out_shape=[jax.ShapeDtypeStruct((size, steps * wide), d) for d in dtypes],
        compiler_params=PARAMS, cost_estimate=cost(product_us(jobs, steps * wide)), name="product",
    )(offsets, *rows, *weights, *after)


def plain(shards, queries, key_rows, values, decay_codes, segment_ids, norm_gain, out_weight):
    tokens, width = queries.shape
    me = lax.axis_index("seq")
    decay_log = jnp.log1p(-decay_codes.astype(F32) / 65536.0)
    segs = segment_ids.reshape(-1, SPAN)
    prefix, state = shard_state(decay_log, segs, key_rows, values)
    gathered = lax.all_gather(state, "seq", axis=0)
    incoming = incoming_state(me, tokens, decay_log, segs, width, [gathered[s] for s in range(shards - 1)], range(shards - 1))
    places = jnp.arange(tokens // SPAN).astype(jnp.int32)
    rows = [normed(places, i, decay_log, segs, norm_gain[None], incoming, prefix, queries, key_rows, values)
            for i in range(tokens // SPAN)]
    weight = lax.all_gather(out_weight, "seq", axis=1, tiled=True)
    partials = jnp.dot(jnp.concatenate(rows), weight, preferred_element_type=F32)
    return lax.psum_scatter(partials.astype(BF16), "head", scatter_dimension=0, tiled=True)


def finish_kernel(half, off_ref, left, left_back, left_own, right, right_back, right_own, _, out):
    step = pl.program_id(0)

    @pl.when(step < half)
    def _():
        out[...] = (left[...].astype(F32) + left_back[...].astype(F32) + left_own[...]).astype(out.dtype)

    @pl.when(step >= half)
    def _():
        out[...] = (right[...].astype(F32) + right_back[...].astype(F32) + right_own[...]).astype(out.dtype)


def finish(spots, tile, lefts, rights, out, after=()):
    rows, wide = lefts[0].shape
    half = wide // tile
    early = pl.BlockSpec((rows, tile), lambda j, off: (0, jnp.minimum(j, half - 1)))
    late = pl.BlockSpec((rows, tile), lambda j, off: (0, jnp.maximum(j, half) - half))
    return pl.pallas_call(
        ignore(functools.partial(finish_kernel, half), 8, len(after)),
        grid_spec=pltpu.PrefetchScalarGridSpec(
            num_scalar_prefetch=1,
            grid=(2 * half,),
            in_specs=[early] * 3 + [late] * 3 + [pl.BlockSpec(memory_space=pl.ANY)] + anywhere(after),
            out_specs=pl.BlockSpec((rows, tile), lambda j, off: (0, off[j])),
        ),
        out_shape=jax.ShapeDtypeStruct(out.shape, out.dtype),
        input_output_aliases={7: 0},
        compiler_params=PARAMS, cost_estimate=cost(2), name="finish",
    )(spots, *lefts, *rights, out, *after)


def last_finish_kernel(tile, first, off_ref, came, back, own, _, out, sums, done):
    sums[...] = (came[...].astype(F32) + back[...].astype(F32) + own[...]).astype(sums.dtype)
    copies = []
    for t in range(sums.shape[1] // tile):
        place = pl.multiple_of(off_ref[first + t] * tile, tile)
        copies.append(pltpu.make_async_copy(sums.at[:, pl.ds(t * tile, tile)], out.at[:, pl.ds(place, tile)], done.at[t]))
        copies[-1].start()
    for copy in copies:
        copy.wait()


def last_finish(spots, tile, first, parts, out):
    rows, wide = parts[0].shape
    vmem, any_place = pl.BlockSpec(memory_space=pltpu.VMEM), pl.BlockSpec(memory_space=pl.ANY)
    return pl.pallas_call(
        functools.partial(last_finish_kernel, tile, first),
        in_specs=[smem()] + [vmem] * 3 + [any_place],
        out_specs=any_place,
        out_shape=jax.ShapeDtypeStruct(out.shape, out.dtype),
        scratch_shapes=[pltpu.VMEM((rows, wide), out.dtype), pltpu.SemaphoreType.DMA((wide // tile,))],
        input_output_aliases={4: 0},
        compiler_params=PARAMS, cost_estimate=cost(1), name="finish",
    )(spots, *parts, out)


def merge_kernel(a, b, c, d, left, right):
    left[...] = (a[...].astype(F32) + b[...]).astype(BF16)
    right[...] = (c[...].astype(F32) + d[...]).astype(BF16)


def merge(came, own, came_back, own_back, after=()):
    rows, wide = came.shape
    part = pl.BlockSpec((rows, 512), lambda j: (0, j))
    shape = jax.ShapeDtypeStruct(came.shape, BF16)
    return pl.pallas_call(
        ignore(merge_kernel, 4, len(after)),
        grid=(wide // 512,),
        in_specs=[part] * 4 + anywhere(after),
        out_specs=[part] * 2,
        out_shape=[shape, shape],
        compiler_params=PARAMS, cost_estimate=cost(1.5), name="merge",
    )(came, own, came_back, own_back, *after)


def cut_kernel(off_ref, x_ref, most, rest):
    step = pl.program_id(0)

    @pl.when(step < pl.num_programs(0) - 1)
    def _():
        most[...] = x_ref[...]

    @pl.when(step == pl.num_programs(0) - 1)
    def _():
        rest[...] = x_ref[...]


def cut(start, wide, weight, after):
    depth = weight.shape[0]
    return pl.pallas_call(
        ignore(cut_kernel, 2, len(after)),
        grid_spec=pltpu.PrefetchScalarGridSpec(
            num_scalar_prefetch=1,
            grid=(wide // 256,),
            in_specs=[pl.BlockSpec((depth, 256), lambda j, off: (0, off[0] + j))] + anywhere(after),
            out_specs=[pl.BlockSpec((depth, 256), lambda j, off: (0, jnp.minimum(j, wide // 256 - 2))),
                       pl.BlockSpec((depth, 256), lambda j, off: (0, 0))],
        ),
        out_shape=[jax.ShapeDtypeStruct((depth, w), weight.dtype) for w in (wide - 256, 256)],
        compiler_params=ALL_VMEM, cost_estimate=cost(4), name="cut",
    )(start, weight, *after)


def held(xs, after):
    n = len(xs)
    return pl.pallas_call(
        lambda *refs: None,
        in_specs=anywhere(xs) + anywhere(after),
        out_specs=anywhere(xs),
        out_shape=[jax.ShapeDtypeStruct(x.shape, x.dtype) for x in xs],
        input_output_aliases={i: i for i in range(n)},
        compiler_params=ALL_VMEM, cost_estimate=cost(1), name="held",
    )(*xs, *after)


def ringed(queries, key_rows, values, decay_codes, segment_ids, norm_gain, out_weight):
    tokens, width = queries.shape
    me, line, copy = lax.axis_index("seq"), lax.axis_index("head"), lax.axis_index("grp")
    core, chip = me % 2, me // 2
    ways = [lambda x, d=d: lax.ppermute(x, "head", [(i, (i + d) % 4) for i in range(4)]) for d in (1, 3)]
    sibling = lambda x: lax.ppermute(x, "seq", [(0, 1), (1, 0), (2, 3), (3, 2)])
    onward = lambda x: lax.ppermute(x, "seq", [(0, 2), (1, 3)])
    gather = lambda x: lax.all_gather(x, ("grp", "seq"), axis=0)

    depth, columns = out_weight.shape
    half = columns // 2
    cuts = [(0, half // 3 * 2), (half // 3 * 2, half)]
    decay_log = jnp.log1p(-decay_codes.astype(F32) / 65536.0)
    segs = segment_ids.reshape(-1, SPAN)
    gain = norm_gain[None]
    places = jnp.stack([(line + b) % 4 for b in range(4)]).astype(jnp.int32)
    slices = [chip * 2 + core, chip * 2 + 1 - core, (1 - chip) * 2 + core, (1 - chip) * 2 + 1 - core]
    far_offsets = jnp.stack(slices[2:]).astype(jnp.int32)
    start = (copy * (half // 256)).reshape(1).astype(jnp.int32)

    near = sibling(out_weight)
    prefix, state = shard_state(decay_log, segs, key_rows, values)
    state_c = sibling(state)
    state_x = onward(chip_state(core, tokens, decay_log, state, state_c))
    far = [gather(x) for x in held(cut(start, half, out_weight, [state_c, near]), [state_x])]
    incoming = entering_state(core, chip, tokens, decay_log, segs, state_c, state_x, sibling(state_x))
    norm = lambda i, *after: normed(places, i, decay_log, segs, gain, incoming, prefix, queries, key_rows, values, after=after)

    chunks = [(slices[:2], 512, list(range(columns // 512)))]
    for low, high in cuts:
        chunks.append((slices[2:], 256, [t * (half // 256) + i for t in range(2) for i in range(low // 256, high // 256)]))
    rows = {2: norm(2)}
    out = jnp.zeros((SPAN, 4 * columns), BF16)
    last, waiting = rows[2], None
    for number, (owners, tile, tiles) in enumerate(chunks):
        def mul(jobs, dtypes, *after):
            used = sorted({r for r, _ in jobs})
            where = [(used.index(r), side) for r, side in jobs]
            pair = [out_weight, near] if number < 1 else [far[number - 1]] * 2
            return product(far_offsets, where, dtypes, [rows[r] for r in used], pair, after=after)

        across = mul([(2, 0), (2, 1)], [BF16] * 2, last)
        come = [way(x) for way, x in zip(ways, across)]
        if 1 not in rows:
            rows[1] = norm(1, across[1])
            rows[3] = norm(3, rows[1])
        left, right, *mine = mul([(3, 0), (1, 1), (1, 0), (3, 1)], [BF16, BF16, F32, F32], across[0], rows[3])
        straight = [ways[1](left), ways[0](right)]
        if 0 not in rows:
            rows[0] = norm(0, left)
        own = mul([(0, 0), (0, 1)], [F32] * 2, left)
        if waiting is not None:
            out = waiting(out, own[0])
        sums = merge(come[0], mine[0], come[1], mine[1], after=[own[0], out])
        last = sums[0]
        sums = [way(x) for way, x in zip(ways, sums)]
        spots = jnp.stack([owner * (columns // tile) + t for owner in owners for t in tiles]).astype(jnp.int32)

        def waiting(out, after, spots=spots, tile=tile, sums=sums, straight=straight, own=own):
            return finish(spots, tile, [sums[0], straight[0], own[0]], [straight[1], sums[1], own[1]], out, after=[after])

    out = last_finish(spots, tile, 0, [sums[0], straight[0], own[0]], out)
    return last_finish(spots, tile, len(tiles), [straight[1], sums[1], own[1]], out)


def per_device(sizes, *args):
    if sizes == (2, 4, 4) and args[-1].shape[1] == 1536:
        return ringed(*args)
    return plain(sizes[1], *args)


def solution(mesh):
    in_specs = (
        P(("grp", "seq"), "head"),
        P(("grp", "seq"), "head"),
        P(("grp", "seq"), "head"),
        P("head"),
        P(("grp", "seq")),
        P("head"),
        P("head", "seq"),
    )
    out_specs = P(("grp", "seq", "head"), None)
    sizes = (mesh.shape["grp"], mesh.shape["seq"], mesh.shape["head"])
    return jax.shard_map(
        functools.partial(per_device, sizes), mesh=mesh, in_specs=in_specs, out_specs=out_specs, check_vma=False
    )
```
